32 devices in a mesh: ctx: 8 (over z, y), fsdp: 4 (over x, core).
Axes of the slice: x: 2, y: 2, z: 4, core: 2. Of those that a mesh axis runs over, the one named last changes fastest.
Arguments:
- hidden_in: bfloat16 [4, 2048, 4096], P('fsdp', 'ctx'), may hold values from -40 to 40
- page_tokens: int32 [4, 8], P('fsdp'), may hold values from 1 to 1024, 2048 in all within a row
- grad_attn: bfloat16 [4, 2048, 128], P('fsdp', 'ctx'), may hold values from -6 to 6
- w_qkv: bfloat16 [4096, 384], P('fsdp'), may hold values from -1 to 1
Outputs:
- grad_hidden: bfloat16 [4, 2048, 4096], P('fsdp', 'ctx')
- grad_w_qkv: float32 [4096, 384], P('fsdp')
The draws below stay inside these ranges and needn't reach their ends.
Inputs may be any that keep to these rules, and one draw needn't show every extreme that they name: `page_tokens`: each document's page lengths sum to 2048.
All inputs are finite; a program needn't handle non-finite values.
Results may differ from the reference program's by a relative error of at most 0.039.
Values may be sent and summed in bfloat16 or wider, within the bound.
No kernel may reach another device: no remote copies, remote signals or barrier semaphores. Data moves between devices by JAX's collectives and lax.ppermute only.
A program may use at most 128 MiB of HBM per device.

```python
import math
import jax
import jax.numpy as jnp
import numpy as np
from jax import lax

D = 4096
HD = 128
QH = 1
TOK_DEV = 256
SEQ = 2048
DOCS = 4
PAGES = 8
PAGE_MOST = 1024
N_CTX = 8


def draw_hidden_in(key, part):
    values_drawn = jax.random.truncated_normal(key, -4.0, 4.0, (DOCS, SEQ, D), jnp.float32)
    pairing = jax.random.permutation(jax.random.fold_in(key, 5), N_CTX).astype(jnp.int32)
    block_of_row = jnp.arange(SEQ, dtype=jnp.int32) // TOK_DEV
    group_of_col = jnp.arange(D, dtype=jnp.int32) // (D // N_CTX)
    heavy = pairing[block_of_row][:, None] == group_of_col[None, :]
    values_drawn = values_drawn * jnp.where(heavy, 5.0, 1.0)[None, :, :]
    return values_drawn.astype(jnp.bfloat16)


def draw_w_qkv(key, part):
    values_drawn = jax.random.truncated_normal(key, -3.0, 3.0, (D, (QH + 2) * HD), jnp.float32) * D ** (-0.5)
    return values_drawn.astype(jnp.bfloat16)


def block_scale(stream_key, extent, cuts, smallest, high):
    factor_of, own = 1.0, jax.random.fold_in(stream_key, 6)
    for dim, parts in cuts:
        heights = jnp.exp(jax.random.uniform(jax.random.fold_in(own, dim), (parts,), jnp.float32, smallest / len(cuts), high / len(cuts)))
        factor_of = factor_of * jnp.repeat(heights, extent[dim] // parts).reshape([-1 if axis == dim else 1 for axis in range(len(extent))])
    return factor_of


def length_profile(amount, total, most, skew):
    portions = [(1 << 20) // math.isqrt(standing ** skew) + 1 for standing in range(2, amount + 1)]
    spare, holding = total - most - (amount - 1), [1] * (amount - 1)
    while spare > 0:
        free = [i for i in range(amount - 1) if holding[i] < most]
        pool, remaining = sum([portions[i] for i in free]), spare
        for i in free:
            extra = min(most - holding[i], max(1, remaining * portions[i] // pool), spare)
            holding[i] = holding[i] + extra
            spare = spare - extra
    return np.array([most] + holding)


def ragged_sizes(key, amount, total, bound, slope):
    if amount == 2:
        one = jax.random.randint(key, (), max(1, total - bound), min(bound, total - 1) + 1)
        return jnp.stack([one, total - one])
    sizes = jnp.asarray(length_profile(amount, total, bound, slope), jnp.int32)
    pairs = (amount - 1) // 2
    donor, receiver = sizes[1:1 + 2 * pairs:2], sizes[2:2 + 2 * pairs:2]
    room = jnp.minimum(donor - 1, bound - receiver)
    moved = jax.random.randint(jax.random.fold_in(key, 1), (pairs,), 0, 1 << 20) % (room + 1)
    sizes = sizes.at[1:1 + 2 * pairs:2].set(donor - moved).at[2:2 + 2 * pairs:2].set(receiver + moved)
    return sizes[jax.random.permutation(jax.random.fold_in(key, 2), amount)]


def noise(own_key, extent, deviation, bound, cuts=(), kind=jnp.bfloat16):
    drawn = jax.random.normal(own_key, extent, jnp.float32) * deviation
    if len(cuts) > 0:
        drawn = block_scale(own_key, extent, cuts, -0.22, 0.18) * drawn
    return jnp.clip(drawn, min=-bound, max=bound).astype(kind)


def setup_inputs(seed: int = 0) -> dict:
    streams_of = jax.random.split(jax.random.key(seed), 5)
    hidden_in = draw_hidden_in(jax.random.fold_in(streams_of[4], 71), 0)
    page_tokens = jax.vmap(lambda own: ragged_sizes(own, PAGES, SEQ, PAGE_MOST, 1))(jax.random.split(streams_of[1], DOCS)).reshape((DOCS, PAGES)).astype(jnp.int32)
    grad_attn = noise(streams_of[2], (DOCS, SEQ, QH * HD), 1.0, 6.0, ((0, 4), (1, 8)))
    w_qkv = draw_w_qkv(jax.random.fold_in(streams_of[4], 71), 0)
    return dict(hidden_in=hidden_in, page_tokens=page_tokens, grad_attn=grad_attn, w_qkv=w_qkv)


def page_limits(page_row, positions, total_len):
    page_ends = jnp.cumsum(page_row).astype(jnp.int32)
    return jnp.min(jnp.where(page_ends[None, :] > positions[:, None], page_ends[None, :], total_len), axis=1)


def reference(hidden_in, page_tokens, grad_attn, w_qkv):
    score_scale = HD ** -0.5

    def one_doc(doc_args):
        inputs_doc, page_row, grad_out = doc_args
        projected = jnp.dot(inputs_doc, w_qkv, preferred_element_type=jnp.float32).astype(jnp.bfloat16)
        queries = projected[:, :HD]
        keys_all = projected[:, HD:2 * HD]
        values_all = projected[:, 2 * HD:]
        key_pos = jnp.arange(SEQ, dtype=jnp.int32)
        limits = page_limits(page_row, key_pos, SEQ)
        visible = key_pos[None, :] < limits[:, None]
        scores = jnp.where(visible, jnp.dot(queries, keys_all.T, preferred_element_type=jnp.float32) * score_scale, -1e30)
        row_max = jnp.max(scores, axis=1, keepdims=True)
        log_total = row_max[:, 0] + jnp.log(jnp.sum(jnp.exp(scores - row_max), axis=1))
        probs_full = jnp.exp(scores - log_total[:, None])
        probs_half = probs_full.astype(jnp.bfloat16)
        attended = jnp.dot(probs_half, values_all, preferred_element_type=jnp.float32)
        out_dot = jnp.sum(grad_out.astype(jnp.float32) * attended, axis=1)
        dprob = jnp.dot(grad_out, values_all.T, preferred_element_type=jnp.float32)
        dscore = (probs_full * (dprob - out_dot[:, None]) * score_scale).astype(jnp.bfloat16)
        query_grad = jnp.dot(dscore, keys_all, preferred_element_type=jnp.float32)
        key_grad = jnp.dot(dscore.T, queries, preferred_element_type=jnp.float32)
        value_grad = jnp.dot(probs_half.T, grad_out, preferred_element_type=jnp.float32)
        grad_qkv = jnp.concatenate([query_grad, key_grad, value_grad], axis=1).astype(jnp.bfloat16)
        grad_inputs = jnp.dot(grad_qkv, w_qkv.T, preferred_element_type=jnp.float32).astype(jnp.bfloat16)
        blocks_in = inputs_doc.reshape(N_CTX, TOK_DEV, D)
        blocks_grad = grad_qkv.reshape(N_CTX, TOK_DEV, (QH + 2) * HD)

        def block_step(running, block_pair):
            block_term = jnp.dot(block_pair[0].T, block_pair[1], preferred_element_type=jnp.float32).astype(jnp.bfloat16)
            return running + lax.optimization_barrier(block_term).astype(jnp.float32), None

        weight_sum, _ = lax.scan(block_step, jnp.zeros((D, (QH + 2) * HD), jnp.float32), (blocks_in, blocks_grad))
        return grad_inputs, weight_sum

    grad_hidden, weight_terms = lax.map(one_doc, (hidden_in, page_tokens, grad_attn))
    return grad_hidden, jnp.sum(weight_terms, axis=0)
```

```python
import functools
import math

import jax
import jax.numpy as jnp
from jax import lax
from jax.experimental import pallas as pl
from jax.experimental.pallas import tpu as pltpu
from jax.sharding import PartitionSpec as P

F32 = jnp.float32
BF16 = jnp.bfloat16
VMEM = pl.BlockSpec(memory_space=pltpu.VMEM)
SMEM = pl.BlockSpec(memory_space=pltpu.SMEM)
PARAMS = pltpu.CompilerParams(vmem_limit_bytes=56 * 1024 * 1024)


def nt(left, right):
    return lax.dot_general(left, right, (((1,), (1,)), ((), ())), preferred_element_type=F32)


def nn(left, right):
    return jnp.dot(left, right, preferred_element_type=F32)


def tn(left, right):
    return lax.dot_general(left, right, (((0,), (0,)), ((), ())), preferred_element_type=F32)


def project_kernel(parts, ids_ref, hidden_ref, *refs):
    weights, out_ref = refs[:parts], refs[parts]
    rows = weights[0].shape[0]
    total = None
    for part in range(parts):
        start = pl.multiple_of(ids_ref[part] * rows, rows)
        term = nn(hidden_ref[:, pl.ds(start, rows)], weights[part][...])
        total = term if total is None else total + term
    out_ref[...] = total.astype(BF16)


def project(ids, hidden, weights):
    return pl.pallas_call(
        functools.partial(project_kernel, len(weights)),
        out_shape=jax.ShapeDtypeStruct((hidden.shape[0], weights[0].shape[1]), BF16),
        in_specs=[SMEM] + [VMEM] * (1 + len(weights)),
        out_specs=VMEM,
        compiler_params=PARAMS,
        cost_estimate=pl.CostEstimate(
            flops=2 * hidden.size * weights[0].shape[1], bytes_accessed=4 * hidden.size, transcendentals=0
        ),
        name="project",
    )(ids, hidden, *weights)


def hidden_kernel(parts, ids_ref, grad_ref, *refs):
    weights, out_ref = refs[:parts], refs[parts]
    rows = weights[0].shape[0]
    for part in range(parts):
        start = pl.multiple_of(ids_ref[part] * rows, rows)
        out_ref[:, pl.ds(start, rows)] = nt(grad_ref[...], weights[part][...]).astype(BF16)


def hidden_grad(ids, grad, weights):
    width = len(weights) * weights[0].shape[0]
    return pl.pallas_call(
        functools.partial(hidden_kernel, len(weights)),
        out_shape=jax.ShapeDtypeStruct((grad.shape[0], width), BF16),
        in_specs=[SMEM] + [VMEM] * (1 + len(weights)),
        out_specs=VMEM,
        compiler_params=PARAMS,
        cost_estimate=pl.CostEstimate(
            flops=2 * grad.size * width, bytes_accessed=4 * grad.shape[0] * width, transcendentals=0
        ),
        name="hidden_grad",
    )(ids, grad, *weights)


def attend_kernel(blocks, bq, bk, ids_ref, pages_ref, *refs):
    qkv_parts, out_parts = refs[:blocks], refs[blocks : 2 * blocks]
    grad_ref, own_ref = refs[2 * blocks : 2 * blocks + 2]
    qkv_ref, do_ref, s_ref, dp_ref, dk_ref, dv_ref, kt_ref = refs[2 * blocks + 2 :]
    seq, hd = do_ref.shape
    rows = seq // blocks
    scale = hd**-0.5
    scale2 = scale * math.log2(math.e)
    for block in range(blocks):
        start = pl.multiple_of(ids_ref[block] * rows, rows)
        qkv_ref[pl.ds(start, rows), :] = qkv_parts[block][...]
        do_ref[pl.ds(start, rows), :] = out_parts[block][:, out_parts[block].shape[1] - hd :]
    dk_ref[...] = jnp.zeros_like(dk_ref)
    dv_ref[...] = jnp.zeros_like(dv_ref)
    kt_ref[...] = qkv_ref[:, hd : 2 * hd].T
    ends, end = [], jnp.int32(0)
    for page in range(pages_ref.shape[1]):
        end = end + pages_ref[0, page]
        ends.append(end)

    def limit_of(pos):
        limit = jnp.full_like(pos, seq)
        for page_end in ends:
            limit = jnp.minimum(limit, jnp.where(page_end > pos, page_end, seq))
        return limit

    @pl.loop(0, seq // bq)
    def _(i):
        q0 = pl.multiple_of(i * bq, bq)
        limits = limit_of(q0 + lax.broadcasted_iota(jnp.int32, (1, bq), 1))
        count = lax.div(limit_of(q0 + (bq - 1)) + (bk - 1), bk)
        q = qkv_ref[pl.ds(q0, bq), :hd]
        do = do_ref[pl.ds(q0, bq), :]

        def scores(j, row_max):
            k0 = pl.multiple_of(j * bk, bk)
            s = nt(qkv_ref[pl.ds(k0, bk), hd : 2 * hd], q) * scale2
            key = k0 + lax.broadcasted_iota(jnp.int32, (bk, 1), 0)
            s = jnp.where(key < limits, s, -1e30)
            s_ref[pl.ds(k0, bk), :] = s
            dp_ref[pl.ds(k0, bk), :] = nt(qkv_ref[pl.ds(k0, bk), 2 * hd :], do)
            return jnp.maximum(row_max, jnp.max(s, axis=0, keepdims=True))

        row_max = lax.fori_loop(0, count, scores, jnp.full((1, bq), -3e38, F32))

        def sums(j, carry):
            total, dot = carry
            k0 = pl.multiple_of(j * bk, bk)
            p = jnp.exp2(s_ref[pl.ds(k0, bk), :] - row_max)
            s_ref[pl.ds(k0, bk), :] = p
            total = total + jnp.sum(p, axis=0, keepdims=True)
            dot = dot + jnp.sum(p * dp_ref[pl.ds(k0, bk), :], axis=0, keepdims=True)
            return total, dot

        zero = jnp.zeros((1, bq), F32)
        total, dot = lax.fori_loop(0, count, sums, (zero, zero))
        inv = 1.0 / total
        gain = inv * scale
        shift = dot * inv * gain

        def grads(j, dqt):
            k0 = pl.multiple_of(j * bk, bk)
            p = s_ref[pl.ds(k0, bk), :]
            half = (p * inv).astype(BF16)
            ds = (p * (dp_ref[pl.ds(k0, bk), :] * gain - shift)).astype(BF16)
            dv_ref[pl.ds(k0, bk), :] += nn(half, do)
            dk_ref[pl.ds(k0, bk), :] += nn(ds, q)
            return dqt + nn(kt_ref[:, pl.ds(k0, bk)], ds)

        dqt = lax.fori_loop(0, count, grads, jnp.zeros((hd, bq), F32))
        grad_ref[pl.ds(q0, bq), :hd] = dqt.T.astype(BF16)

    grad_ref[:, hd : 2 * hd] = dk_ref[...].astype(BF16)
    grad_ref[:, 2 * hd :] = dv_ref[...].astype(BF16)
    own = pl.multiple_of(ids_ref[0] * rows, rows)
    own_ref[...] = grad_ref[pl.ds(own, rows), :]


def attend(ids, pages, qkv_parts, out_parts, hd):
    blocks = len(qkv_parts)
    rows, width = qkv_parts[0].shape
    seq = rows * blocks
    block = 512 if seq % 512 == 0 and seq <= 4096 else rows
    return pl.pallas_call(
        functools.partial(attend_kernel, blocks, block, block),
        out_shape=(jax.ShapeDtypeStruct((seq, width), BF16), jax.ShapeDtypeStruct((rows, width), BF16)),
        in_specs=[SMEM, SMEM] + [VMEM] * (2 * blocks),
        out_specs=(VMEM, VMEM),
        scratch_shapes=[
            pltpu.VMEM((seq, width), BF16),
            pltpu.VMEM((seq, hd), BF16),
            pltpu.VMEM((seq, block), F32),
            pltpu.VMEM((seq, block), F32),
            pltpu.VMEM((seq, hd), F32),
            pltpu.VMEM((seq, hd), F32),
            pltpu.VMEM((hd, seq), BF16),
        ],
        compiler_params=PARAMS,
        cost_estimate=pl.CostEstimate(
            flops=10 * seq * seq * hd, bytes_accessed=6 * seq * width, transcendentals=seq * seq
        ),
        name="attend",
    )(ids, pages, *qkv_parts, *out_parts)


def weight_kernel(blocks, ids_ref, grad_ref, *refs):
    hidden_parts, out_ref = refs[:blocks], refs[blocks]
    rows = grad_ref.shape[0] // blocks
    total = None
    for block in range(blocks):
        start = pl.multiple_of(ids_ref[block] * rows, rows)
        term = tn(hidden_parts[block][:, : out_ref.shape[0]], grad_ref[pl.ds(start, rows), :])
        total = term if total is None else total + term
    out_ref[...] = total


def weight_grad(ids, grad, hidden_parts, columns):
    return pl.pallas_call(
        functools.partial(weight_kernel, len(hidden_parts)),
        out_shape=jax.ShapeDtypeStruct((columns, grad.shape[1]), F32),
        in_specs=[SMEM] + [VMEM] * (1 + len(hidden_parts)),
        out_specs=VMEM,
        compiler_params=PARAMS,
        cost_estimate=pl.CostEstimate(
            flops=2 * grad.size * columns, bytes_accessed=4 * grad.shape[0] * columns, transcendentals=0
        ),
        name="weight_grad",
    )(ids, grad, *hidden_parts)


def swap(array, axis, size, distance):
    return lax.ppermute(array, axis, [(i, i ^ distance) for i in range(size)])


def local(ctx_size, fsdp_size, hidden_in, page_tokens, grad_attn, w_qkv):
    hidden, grad_out = hidden_in[0], grad_attn[0]
    rows, depth = hidden.shape
    hd = grad_out.shape[1]
    f, c = lax.axis_index("fsdp"), lax.axis_index("ctx")
    fsdp_ids = f ^ jnp.arange(fsdp_size, dtype=jnp.int32)
    ctx_ids = c ^ jnp.arange(ctx_size, dtype=jnp.int32)
    piece = depth // (fsdp_size * ctx_size)
    columns = fsdp_size * piece

    weights = {0: w_qkv}
    bit = fsdp_size // 2
    while bit:
        weights.update({k ^ bit: swap(weights[k], "fsdp", fsdp_size, bit) for k in list(weights)})
        bit //= 2
    weights = [weights[k] for k in range(fsdp_size)]

    cut = hidden.reshape(rows, fsdp_size, ctx_size, piece)
    hidden_parts = []
    for k in range(ctx_size):
        chunk = lax.dynamic_index_in_dim(cut, ctx_ids[k], 2, keepdims=False).reshape(rows, columns)
        chunk = jnp.concatenate([chunk, grad_out], axis=1)
        hidden_parts.append(swap(chunk, "ctx", ctx_size, k) if k else chunk)

    projected = project(fsdp_ids, hidden, weights)
    qkv_parts = [swap(projected, "ctx", ctx_size, k) if k else projected for k in range(ctx_size)]
    grad_all, grad_own = attend(ctx_ids, page_tokens, qkv_parts, hidden_parts, hd)
    partial = weight_grad(ctx_ids, grad_all, hidden_parts, columns)
    grad_inputs = hidden_grad(fsdp_ids, grad_own, weights)

    partial = partial.reshape(fsdp_size, piece, -1)
    bit = 1
    while bit < fsdp_size:
        pairs = partial.reshape(partial.shape[0] // 2, 2, *partial.shape[1:])
        mine = (f // bit) % 2
        away = lax.dynamic_index_in_dim(pairs, 1 - mine, 1, keepdims=False).astype(BF16)
        kept = lax.dynamic_index_in_dim(pairs, mine, 1, keepdims=False)
        partial = kept + swap(away, "fsdp", fsdp_size, bit).astype(F32)
        bit *= 2
    reduced = partial[0].astype(BF16)
    copies = jnp.broadcast_to(reduced[None], (ctx_size, *reduced.shape))
    gathered = lax.all_to_all(copies, "ctx", 0, 0)
    grad_weights = gathered.reshape(ctx_size * piece, -1).astype(F32)
    return grad_inputs[None], grad_weights


def solution(mesh):
    in_specs = (P("fsdp", "ctx", None), P("fsdp", None), P("fsdp", "ctx", None), P("fsdp", None))
    out_specs = (P("fsdp", "ctx", None), P("fsdp", None))
    body = functools.partial(local, mesh.shape["ctx"], mesh.shape["fsdp"])
    return jax.shard_map(body, mesh=mesh, in_specs=in_specs, out_specs=out_specs, check_vma=False)
```

```python
import functools
import math

import jax
import jax.numpy as jnp
from jax import lax
from jax.experimental import pallas as pl
from jax.experimental.pallas import tpu as pltpu
from jax.sharding import PartitionSpec as P

F32 = jnp.float32
BF16 = jnp.bfloat16
VMEM = pl.BlockSpec(memory_space=pltpu.VMEM)
SMEM = pl.BlockSpec(memory_space=pltpu.SMEM)
PARAMS = pltpu.CompilerParams(vmem_limit_bytes=56 * 1024 * 1024)


def nt(left, right):
    return lax.dot_general(left, right, (((1,), (1,)), ((), ())), preferred_element_type=F32)


def nn(left, right):
    return jnp.dot(left, right, preferred_element_type=F32)


def tn(left, right):
    return lax.dot_general(left, right, (((0,), (0,)), ((), ())), preferred_element_type=F32)


def pallas(kernel, out_shape, scalars, arrays, name, flops, scratch=()):
    outs = out_shape if isinstance(out_shape, tuple) else (out_shape,)
    moved = sum(a.size * a.dtype.itemsize for a in (*arrays, *outs))
    return pl.pallas_call(
        kernel,
        out_shape=out_shape,
        in_specs=[SMEM] * len(scalars) + [VMEM] * len(arrays),
        out_specs=jax.tree.map(lambda _: VMEM, out_shape),
        scratch_shapes=scratch,
        compiler_params=PARAMS,
        cost_estimate=pl.CostEstimate(flops=flops, bytes_accessed=moved, transcendentals=0),
        name=name,
    )(*scalars, *arrays)


def shape(dims, dtype=BF16):
    return jax.ShapeDtypeStruct(dims, dtype)


def cut_kernel(group, fsdp_size, ctx_size, piece, ids_ref, hidden_ref, *outs):
    for k, out in enumerate(outs):
        for block in range(fsdp_size * ctx_size // group):
            start = pl.multiple_of((block * group + ids_ref[k]) * piece, piece)
            out[:, block * piece : (block + 1) * piece] = hidden_ref[:, pl.ds(start, piece)]


def cut(ids, hidden, group, fsdp_size, ctx_size):
    rows, depth = hidden.shape
    piece = depth // (fsdp_size * ctx_size)
    if piece % 128:
        pieces = hidden.reshape(rows, depth // (piece * group), group, piece)
        return [
            lax.dynamic_index_in_dim(pieces, ids[k], 2, keepdims=False).reshape(rows, depth // group)
            for k in range(group)
        ]
    return pallas(
        functools.partial(cut_kernel, group, fsdp_size, ctx_size, piece),
        tuple(shape((rows, depth // group)) for _ in range(group)),
        [ids],
        [hidden],
        "cut",
        0,
    )


def project_kernel(columns, width, ids_ref, hidden_ref, *refs):
    out_ref = refs[len(columns)]
    total = None
    for part, first in enumerate(columns):
        weight = refs[part]
        rows = weight.shape[0]
        start = pl.multiple_of(ids_ref[part] * rows, rows)
        term = nn(hidden_ref[:, pl.ds(start, rows)], weight[:, first : first + width])
        total = term if total is None else total + term
    out_ref[...] = total.astype(BF16)


def project(ids, hidden, parts, width):
    return pallas(
        functools.partial(project_kernel, [first for _, first in parts], width),
        shape((hidden.shape[0], width)),
        [ids],
        [hidden] + [array for array, _ in parts],
        "project",
        2 * hidden.size * width,
    )


def hidden_kernel(layout, ids_ref, grad_ref, *refs):
    out_ref = refs[len(refs) - 1]
    at = 0
    for part, pieces in enumerate(layout):
        total = None
        for first, count in pieces:
            weight = refs[at]
            at += 1
            rows = weight.shape[0]
            term = nt(grad_ref[:, first : first + count], weight[...])
            total = term if total is None else total + term
        start = pl.multiple_of(ids_ref[part] * rows, rows)
        out_ref[:, pl.ds(start, rows)] = total.astype(BF16)


def hidden_grad(ids, grad, layout, weights, depth):
    return pallas(
        functools.partial(hidden_kernel, layout),
        shape((grad.shape[0], depth)),
        [ids],
        [grad, *weights],
        "hidden_grad",
        2 * grad.size * depth,
    )


def attend_kernel(blocks, group, bq, bk, ids_ref, pages_ref, *refs):
    q_parts, k_parts, v_parts, g_parts = (refs[i * blocks : (i + 1) * blocks] for i in range(4))
    grad_ref, own_ref = refs[4 * blocks : 4 * blocks + 2]
    q_ref, k_ref, v_ref, do_ref, s_ref, dp_ref, dk_ref, dv_ref, kt_ref = refs[4 * blocks + 2 :]
    seq, hd = do_ref.shape
    rows = seq // blocks
    near = rows * group
    scale = hd**-0.5
    scale2 = scale * math.log2(math.e)
    for block in range(blocks):
        here = pl.ds(pl.multiple_of(ids_ref[block] * rows, rows), rows)
        q_ref[here, :] = q_parts[block][...]
        k_ref[here, :] = k_parts[block][...]
        v_ref[here, :] = v_parts[block][...]
        do_ref[here, :] = g_parts[block][...]
    dk_ref[...] = jnp.zeros_like(dk_ref)
    dv_ref[...] = jnp.zeros_like(dv_ref)
    kt_ref[...] = k_ref[...].T
    ends, end = [], jnp.int32(0)
    for page in range(pages_ref.shape[1]):
        end = end + pages_ref[0, page]
        ends.append(end)
    low = lax.div(ids_ref[0], group) * near
    near_first, near_last = lax.div(low, bk), lax.div(low, bk) + near // bk

    def limit_of(pos):
        limit = jnp.full_like(pos, seq)
        for page_end in ends:
            limit = jnp.minimum(limit, jnp.where(page_end > pos, page_end, seq))
        return limit

    @pl.loop(0, seq // bq)
    def _(i):
        q0 = pl.multiple_of(i * bq, bq)
        limits = limit_of(q0 + lax.broadcasted_iota(jnp.int32, (1, bq), 1))
        count = lax.div(limit_of(q0 + (bq - 1)) + (bk - 1), bk)
        q = q_ref[pl.ds(q0, bq), :]
        do = do_ref[pl.ds(q0, bq), :]

        def scores(j, row_max):
            k0 = pl.multiple_of(j * bk, bk)
            s = nt(k_ref[pl.ds(k0, bk), :], q) * scale2
            key = k0 + lax.broadcasted_iota(jnp.int32, (bk, 1), 0)
            s = jnp.where(key < limits, s, -1e30)
            s_ref[pl.ds(k0, bk), :] = s
            dp_ref[pl.ds(k0, bk), :] = nt(v_ref[pl.ds(k0, bk), :], do)
            return jnp.maximum(row_max, jnp.max(s, axis=0, keepdims=True))

        row_max = lax.fori_loop(0, count, scores, jnp.full((1, bq), -3e38, F32))

        def sums(j, carry):
            total, dot = carry
            k0 = pl.multiple_of(j * bk, bk)
            p = jnp.exp2(s_ref[pl.ds(k0, bk), :] - row_max)
            s_ref[pl.ds(k0, bk), :] = p
            total = total + jnp.sum(p, axis=0, keepdims=True)
            dot = dot + jnp.sum(p * dp_ref[pl.ds(k0, bk), :], axis=0, keepdims=True)
            return total, dot

        zero = jnp.zeros((1, bq), F32)
        total, dot = lax.fori_loop(0, count, sums, (zero, zero))
        inv = 1.0 / total
        gain = inv * scale
        shift = dot * inv * gain

        def dscore(j):
            k0 = pl.multiple_of(j * bk, bk)
            p = s_ref[pl.ds(k0, bk), :]
            return k0, p, (p * (dp_ref[pl.ds(k0, bk), :] * gain - shift)).astype(BF16)

        def key_grads(j, carry):
            k0, p, ds = dscore(j)
            dv_ref[pl.ds(k0 - low, bk), :] += nn((p * inv).astype(BF16), do)
            dk_ref[pl.ds(k0 - low, bk), :] += nn(ds, q)
            return carry

        def query_grads(j, dqt):
            k0, _, ds = dscore(j)
            return dqt + nn(kt_ref[:, pl.ds(k0, bk)], ds)

        def all_grads(j, dqt):
            k0, p, ds = dscore(j)
            dv_ref[pl.ds(k0 - low, bk), :] += nn((p * inv).astype(BF16), do)
            dk_ref[pl.ds(k0 - low, bk), :] += nn(ds, q)
            return dqt + nn(kt_ref[:, pl.ds(k0, bk)], ds)

        first, last = jnp.minimum(near_first, count), jnp.minimum(near_last, count)
        is_near = (q0 >= low) & (q0 < low + near)

        @pl.when(is_near)
        def _():
            dqt = lax.fori_loop(0, first, query_grads, jnp.zeros((hd, bq), F32))
            dqt = lax.fori_loop(first, last, all_grads, dqt)
            dqt = lax.fori_loop(last, count, query_grads, dqt)
            grad_ref[pl.ds(pl.multiple_of(q0 - low, bq), bq), :hd] = dqt.T.astype(BF16)

        @pl.when(jnp.logical_not(is_near))
        def _():
            lax.fori_loop(first, last, key_grads, 0)

    grad_ref[:, hd : 2 * hd] = dk_ref[...].astype(BF16)
    grad_ref[:, 2 * hd :] = dv_ref[...].astype(BF16)
    own = pl.multiple_of(lax.rem(ids_ref[0], group) * rows, rows)
    own_ref[...] = grad_ref[pl.ds(own, rows), :]


def attend(ids, pages, q, k, v, g, group):
    blocks = len(q)
    rows, hd = q[0].shape
    seq = rows * blocks
    near = rows * group
    block = 512 if near % 512 == 0 and seq <= 4096 else rows
    return pallas(
        functools.partial(attend_kernel, blocks, group, block, block),
        (shape((near, 3 * hd)), shape((rows, 3 * hd))),
        [ids, pages],
        [*q, *k, *v, *g],
        "attend",
        10 * seq * seq * hd,
        [pltpu.VMEM((seq, hd), BF16)] * 4
        + [pltpu.VMEM((seq, block), F32)] * 2
        + [pltpu.VMEM((near, hd), F32)] * 2
        + [pltpu.VMEM((hd, seq), BF16)],
    )


def weight_kernel(group, fsdp_size, ids_ref, fsdp_ref, grad_ref, *refs):
    parts, (kept_ref, away_ref) = refs[:group], refs[group:]
    rows = grad_ref.shape[0] // group
    size = parts[0].shape[1] // fsdp_size
    for j in range(fsdp_size):
        columns = pl.ds(pl.multiple_of(fsdp_ref[j] * size, size), size)
        total = None
        for k in range(group):
            here = pl.ds(pl.multiple_of(ids_ref[k] * rows, rows), rows)
            term = tn(parts[k][:, columns], grad_ref[here, :])
            total = term if total is None else total + term
        out = away_ref if j % 2 else kept_ref
        out[j // 2] = total.astype(out.dtype)


def weight_grad(ids, fsdp_ids, grad, parts):
    group, fsdp_size, width = len(parts), fsdp_ids.shape[0], grad.shape[1]
    size = parts[0].shape[1] // fsdp_size
    rows = parts[0].shape[0]
    if size % 128:
        total = sum(
            tn(parts[k], lax.dynamic_slice_in_dim(grad, ids[k] * rows, rows, 0)) for k in range(group)
        ).reshape(fsdp_size, size, width)
        both = jnp.take(total, fsdp_ids, axis=0).reshape(fsdp_size // 2, 2, size, width)
        return both[:, 0], both[:, 1].astype(BF16)
    half = (fsdp_size // 2, size, width)
    return pallas(
        functools.partial(weight_kernel, group, fsdp_size),
        (shape(half, F32), shape(half)),
        [ids, fsdp_ids],
        [grad, *parts],
        "weight_grad",
        2 * grad.size * fsdp_size * size,
    )


def swap(array, axis, size, distance):
    return lax.ppermute(array, axis, [(i, i ^ distance) for i in range(size)])


def gather_blocks(block, size):
    even = [swap(block, "ctx", size, k) if k else block for k in range(0, size, 2)]
    odd = swap(jnp.concatenate(even, axis=0), "ctx", size, 1)
    rows = block.shape[0]
    return even + [odd[i * rows : (i + 1) * rows] for i in range(size // 2)]


def local(ctx_size, fsdp_size, hidden_in, page_tokens, grad_attn, w_qkv):
    hidden, grad_out = hidden_in[0], grad_attn[0]
    rows, depth = hidden.shape
    hd = grad_out.shape[1]
    f, c = lax.axis_index("fsdp"), lax.axis_index("ctx")
    fsdp_ids = f ^ jnp.arange(fsdp_size, dtype=jnp.int32)
    order = jnp.array([*range(0, ctx_size, 2), *range(1, ctx_size, 2)], jnp.int32)
    ctx_ids = c ^ order
    group = min(4, ctx_size)
    group_ids = (c % group) ^ jnp.arange(group, dtype=jnp.int32)

    firsts = [hd, 2 * hd, 0]
    top = fsdp_size // 2
    parts = {0: [(w_qkv, first) for first in firsts]}
    parts[top] = [(swap(w_qkv[:, first : first + hd], "fsdp", fsdp_size, top), 0) for first in firsts]
    bit = top // 2
    while bit:
        for k in list(parts):
            moved = {}
            for array, _ in parts[k]:
                if id(array) not in moved:
                    moved[id(array)] = swap(array, "fsdp", fsdp_size, bit)
            parts[k ^ bit] = [(moved[id(array)], first) for array, first in parts[k]]
        bit //= 2

    g_parts = gather_blocks(grad_out, ctx_size)
    chunks = cut(group_ids, hidden, group, fsdp_size, ctx_size)
    hidden_parts = [swap(chunks[k], "ctx", ctx_size, k) if k else chunks[k] for k in range(group)]

    gathered = []
    for number in range(3):
        weights = [parts[k][number] for k in range(fsdp_size)]
        gathered.append(gather_blocks(project(fsdp_ids, hidden, weights, hd), ctx_size))
    k_parts, v_parts, q_parts = gathered
    grad_near, grad_own = attend(ctx_ids, page_tokens, q_parts, k_parts, v_parts, g_parts, group)

    layout, weights = [], []
    for k in range(fsdp_size):
        if parts[k][0][0] is parts[k][1][0]:
            layout.append([(0, 3 * hd)])
            weights.append(parts[k][0][0])
        else:
            layout.append([(first, hd) for first in firsts])
            weights.extend(array for array, _ in parts[k])
    grad_inputs = hidden_grad(fsdp_ids, grad_own, layout, weights, depth)

    kept, away = weight_grad(group_ids, fsdp_ids, grad_near, hidden_parts)
    bit = 1
    while bit < fsdp_size:
        total = kept + swap(away, "fsdp", fsdp_size, bit).astype(F32)
        bit *= 2
        if bit < fsdp_size:
            kept, away = total[0::2], total[1::2].astype(BF16)
    total = total[0]
    bit = group
    while bit < ctx_size:
        half = total.astype(BF16)
        total = half.astype(F32) + swap(half, "ctx", ctx_size, bit).astype(F32)
        bit *= 2
    total = total.astype(BF16)
    gathered = jnp.stack([swap(total, "ctx", ctx_size, k) if k else total for k in range(group)])
    gathered = jnp.take(gathered, group_ids, axis=0)
    size = total.shape[0] // (ctx_size // group)
    grad_weights = gathered.reshape(group, ctx_size // group, size, -1).swapaxes(0, 1)
    return grad_inputs[None], grad_weights.reshape(ctx_size * size, -1).astype(F32)


def solution(mesh):
    in_specs = (P("fsdp", "ctx", None), P("fsdp", None), P("fsdp", "ctx", None), P("fsdp", None))
    out_specs = (P("fsdp", "ctx", None), P("fsdp", None))
    body = functools.partial(local, mesh.shape["ctx"], mesh.shape["fsdp"])
    return jax.shard_map(body, mesh=mesh, in_specs=in_specs, out_specs=out_specs, check_vma=False)
```

```python
import functools
import math

import jax
import jax.numpy as jnp
from jax import lax
from jax.experimental import pallas as pl
from jax.experimental.pallas import tpu as pltpu
from jax.sharding import PartitionSpec as P

F32 = jnp.float32
BF16 = jnp.bfloat16
VMEM = pl.BlockSpec(memory_space=pltpu.VMEM)
SMEM = pl.BlockSpec(memory_space=pltpu.SMEM)
ANY = pl.BlockSpec(memory_space=pltpu.HBM)
MIB = 1024 * 1024


def nt(left, right):
    return lax.dot_general(left, right, (((1,), (1,)), ((), ())), preferred_element_type=F32)


def nn(left, right):
    return jnp.dot(left, right, preferred_element_type=F32)


def tn(left, right):
    return lax.dot_general(left, right, (((0,), (0,)), ((), ())), preferred_element_type=F32)


def pallas(kernel, out_shape, scalars, arrays, name, flops, scratch=(), far=()):
    outs = out_shape if isinstance(out_shape, tuple) else (out_shape,)
    moved = sum(a.size * a.dtype.itemsize for a in (*arrays, *far, *outs))
    held = moved + sum(math.prod(a.shape) * jnp.dtype(a.dtype).itemsize for a in scratch)
    return pl.pallas_call(
        kernel,
        out_shape=out_shape,
        in_specs=[SMEM] * len(scalars) + [VMEM] * len(arrays) + [ANY] * len(far),
        out_specs=jax.tree.map(lambda _: VMEM, out_shape),
        scratch_shapes=[*scratch]
        + [pltpu.VMEM(a.shape, a.dtype) for a in far]
        + [pltpu.SemaphoreType.DMA] * len(far),
        compiler_params=pltpu.CompilerParams(vmem_limit_bytes=min(held + 8 * MIB, 60 * MIB)),
        cost_estimate=pl.CostEstimate(flops=flops, bytes_accessed=moved, transcendentals=0),
        name=name,
    )(*scalars, *arrays, *far)


def shape(dims, dtype=BF16):
    return jax.ShapeDtypeStruct(dims, dtype)


def cut_kernel(group, fsdp_size, ctx_size, piece, ids_ref, hidden_ref, *refs):
    blocks = fsdp_size * ctx_size // group
    outs, sems = refs[:group], refs[group]
    copies = []
    for k, out in enumerate(outs):
        for block in range(blocks):
            start = pl.multiple_of((block * group + ids_ref[k]) * piece, piece)
            copies.append(
                pltpu.make_async_copy(
                    hidden_ref.at[:, pl.ds(start, piece)],
                    out.at[:, pl.ds(block * piece, piece)],
                    sems.at[k * blocks + block],
                )
            )
    for copy in copies:
        copy.start()
    for copy in copies:
        copy.wait()


def cut(ids, hidden, group, fsdp_size, ctx_size):
    rows, depth = hidden.shape
    piece = depth // (fsdp_size * ctx_size)
    if piece % 128:
        pieces = hidden.reshape(rows, depth // (piece * group), group, piece)
        return [
            lax.dynamic_index_in_dim(pieces, ids[k], 2, keepdims=False).reshape(rows, depth // group)
            for k in range(group)
        ]
    blocks = fsdp_size * ctx_size
    return pl.pallas_call(
        functools.partial(cut_kernel, group, fsdp_size, ctx_size, piece),
        out_shape=tuple(shape((rows, depth // group)) for _ in range(group)),
        in_specs=[SMEM, ANY],
        out_specs=(VMEM,) * group,
        scratch_shapes=[pltpu.SemaphoreType.DMA((blocks,))],
        compiler_params=pltpu.CompilerParams(vmem_limit_bytes=8 * MIB),
        cost_estimate=pl.CostEstimate(flops=0, bytes_accessed=4 * hidden.size, transcendentals=0),
        name="cut",
    )(ids, hidden)


def fetch(sources, slots):
    count = len(sources)
    copies = [pltpu.make_async_copy(sources[i], slots[i], slots[count + i]) for i in range(count)]
    for copy in copies:
        copy.start()
    return copies


def project_kernel(count, ids_ref, *refs):
    slots = refs[len(refs) - 2 * (count + 1) :]
    copies = fetch(refs[: count + 1], slots)
    hidden = slots[count]
    copies[count].wait()
    total = None
    for part in range(count):
        rows = slots[part].shape[0]
        start = pl.multiple_of(ids_ref[part] * rows, rows)
        copies[part].wait()
        term = nn(hidden[:, pl.ds(start, rows)], slots[part][...])
        total = term if total is None else total + term
    first = 0
    for out in refs[count + 1 : len(refs) - 2 * (count + 1)]:
        width = out.shape[1]
        out[...] = total[:, first : first + width].astype(BF16)
        first += width


def project(ids, hidden, weights, widths):
    return pallas(
        functools.partial(project_kernel, len(weights)),
        tuple(shape((hidden.shape[0], width)) for width in widths),
        [ids],
        [],
        "project",
        2 * hidden.size * sum(widths),
        far=[*weights, hidden],
    )


def hidden_kernel(count, ids_ref, grad_ref, *refs):
    slots = refs[count + 1 :]
    copies = fetch(refs[:count], slots)
    for part in range(count):
        rows = slots[part].shape[0]
        start = pl.multiple_of(ids_ref[part] * rows, rows)
        copies[part].wait()
        refs[count][:, pl.ds(start, rows)] = nt(grad_ref[...], slots[part][...]).astype(BF16)


def hidden_grad(ids, grad, weights, depth):
    return pallas(
        functools.partial(hidden_kernel, len(weights)),
        shape((grad.shape[0], depth)),
        [ids],
        [grad],
        "hidden_grad",
        2 * grad.size * depth,
        far=weights,
    )


def attend_kernel(layouts, group, rows, bq, bk, block_ref, pages_ref, *refs):
    count = sum(len(layout) for layout in layouts)
    parts, (grad_ref, own_ref) = refs[:count], refs[count : count + 2]
    q_ref, k_ref, v_ref, do_ref, s_ref, dp_ref, dk_ref, dv_ref, kt_ref = refs[count + 2 :]
    seq, hd = do_ref.shape
    near = rows * group
    block = block_ref[0]
    scale = hd**-0.5
    scale2 = scale * math.log2(math.e)
    at = 0
    for layout, targets in zip(layouts, ((q_ref, k_ref), (v_ref,), (do_ref,))):
        for distances in layout:
            for number, distance in enumerate(distances):
                here = pl.ds(pl.multiple_of((block ^ distance) * rows, rows), rows)
                for column, target in enumerate(targets):
                    target[here, :] = parts[at][number * rows : (number + 1) * rows, column * hd : (column + 1) * hd]
            at += 1
    dk_ref[...] = jnp.zeros_like(dk_ref)
    dv_ref[...] = jnp.zeros_like(dv_ref)
    kt_ref[...] = k_ref[...].T
    ends, end = [], jnp.int32(0)
    for page in range(pages_ref.shape[1]):
        end = end + pages_ref[0, page]
        ends.append(end)
    low = lax.div(block, group) * near
    near_first, near_last = lax.div(low, bk), lax.div(low, bk) + near // bk

    def limit_of(pos):
        limit = jnp.full_like(pos, seq)
        for page_end in ends:
            limit = jnp.minimum(limit, jnp.where(page_end > pos, page_end, seq))
        return limit

    @pl.loop(0, seq // bq)
    def _(i):
        q0 = pl.multiple_of(i * bq, bq)
        limits = limit_of(q0 + lax.broadcasted_iota(jnp.int32, (1, bq), 1))
        count = lax.div(limit_of(q0 + (bq - 1)) + (bk - 1), bk)
        q = q_ref[pl.ds(q0, bq), :]
        do = do_ref[pl.ds(q0, bq), :]

        def scores(j, row_max):
            k0 = pl.multiple_of(j * bk, bk)
            s = nt(k_ref[pl.ds(k0, bk), :], q) * scale2
            key = k0 + lax.broadcasted_iota(jnp.int32, (bk, 1), 0)
            s = jnp.where(key < limits, s, -1e30)
            s_ref[pl.ds(k0, bk), :] = s
            dp_ref[pl.ds(k0, bk), :] = nt(v_ref[pl.ds(k0, bk), :], do)
            return jnp.maximum(row_max, jnp.max(s, axis=0, keepdims=True))

        row_max = lax.fori_loop(0, count, scores, jnp.full((1, bq), -3e38, F32))

        def sums(j, carry):
            total, dot = carry
            k0 = pl.multiple_of(j * bk, bk)
            p = jnp.exp2(s_ref[pl.ds(k0, bk), :] - row_max)
            s_ref[pl.ds(k0, bk), :] = p
            total = total + jnp.sum(p, axis=0, keepdims=True)
            dot = dot + jnp.sum(p * dp_ref[pl.ds(k0, bk), :], axis=0, keepdims=True)
            return total, dot

        zero = jnp.zeros((1, bq), F32)
        total, dot = lax.fori_loop(0, count, sums, (zero, zero))
        inv = 1.0 / total
        gain = inv * scale
        shift = dot * inv * gain

        def dscore(j):
            k0 = pl.multiple_of(j * bk, bk)
            p = s_ref[pl.ds(k0, bk), :]
            return k0, p, (p * (dp_ref[pl.ds(k0, bk), :] * gain - shift)).astype(BF16)

        def key_grads(j, carry):
            k0, p, ds = dscore(j)
            dv_ref[pl.ds(k0 - low, bk), :] += nn((p * inv).astype(BF16), do)
            dk_ref[pl.ds(k0 - low, bk), :] += nn(ds, q)
            return carry

        def query_grads(j, dqt):
            k0, _, ds = dscore(j)
            return dqt + nn(kt_ref[:, pl.ds(k0, bk)], ds)

        def all_grads(j, dqt):
            k0, p, ds = dscore(j)
            dv_ref[pl.ds(k0 - low, bk), :] += nn((p * inv).astype(BF16), do)
            dk_ref[pl.ds(k0 - low, bk), :] += nn(ds, q)
            return dqt + nn(kt_ref[:, pl.ds(k0, bk)], ds)

        first, last = jnp.minimum(near_first, count), jnp.minimum(near_last, count)
        is_near = (q0 >= low) & (q0 < low + near)

        @pl.when(is_near)
        def _():
            dqt = lax.fori_loop(0, first, query_grads, jnp.zeros((hd, bq), F32))
            dqt = lax.fori_loop(first, last, all_grads, dqt)
            dqt = lax.fori_loop(last, count, query_grads, dqt)
            grad_ref[pl.ds(pl.multiple_of(q0 - low, bq), bq), :hd] = dqt.T.astype(BF16)

        @pl.when(jnp.logical_not(is_near))
        def _():
            lax.fori_loop(first, last, key_grads, 0)

    grad_ref[:, hd : 2 * hd] = dk_ref[...].astype(BF16)
    grad_ref[:, 2 * hd :] = dv_ref[...].astype(BF16)
    own = pl.multiple_of(lax.rem(block, group) * rows, rows)
    own_ref[...] = grad_ref[pl.ds(own, rows), :]


def attend(block, pages, sets, blocks, group):
    rows = sets[0][0][0].shape[0] // len(sets[0][0][1])
    hd = sets[1][0][0].shape[1]
    seq, near = rows * blocks, rows * group
    tile = 512 if near % 512 == 0 and seq <= 4096 else rows
    layouts = [[distances for _, distances in parts] for parts in sets]
    return pallas(
        functools.partial(attend_kernel, layouts, group, rows, tile, tile),
        (shape((near, 3 * hd)), shape((rows, 3 * hd))),
        [block, pages],
        [array for parts in sets for array, _ in parts],
        "attend",
        10 * seq * seq * hd,
        [pltpu.VMEM((seq, hd), BF16)] * 4
        + [pltpu.VMEM((seq, tile), F32)] * 2
        + [pltpu.VMEM((near, hd), F32)] * 2
        + [pltpu.VMEM((hd, seq), BF16)],
    )


def weight_kernel(group, fsdp_size, ids_ref, fsdp_ref, grad_ref, *refs):
    parts, (kept_ref, away_ref) = refs[:group], refs[group:]
    rows = grad_ref.shape[0] // group
    size = parts[0].shape[1] // fsdp_size
    for j in range(fsdp_size):
        columns = pl.ds(pl.multiple_of(fsdp_ref[j] * size, size), size)
        total = None
        for k in range(group):
            here = pl.ds(pl.multiple_of(ids_ref[k] * rows, rows), rows)
            term = tn(parts[k][:, columns], grad_ref[here, :])
            total = term if total is None else total + term
        out = away_ref if j % 2 else kept_ref
        out[j // 2] = total.astype(out.dtype)


def weight_grad(ids, fsdp_ids, grad, parts):
    group, fsdp_size, width = len(parts), fsdp_ids.shape[0], grad.shape[1]
    size = parts[0].shape[1] // fsdp_size
    rows = parts[0].shape[0]
    if size % 128:
        total = sum(
            tn(parts[k], lax.dynamic_slice_in_dim(grad, ids[k] * rows, rows, 0)) for k in range(group)
        ).reshape(fsdp_size, size, width)
        both = jnp.take(total, fsdp_ids, axis=0).reshape(fsdp_size // 2, 2, size, width)
        return both[:, 0], both[:, 1].astype(BF16)
    half = (fsdp_size // 2, size, width)
    return pallas(
        functools.partial(weight_kernel, group, fsdp_size),
        (shape(half, F32), shape(half)),
        [ids, fsdp_ids],
        [grad, *parts],
        "weight_grad",
        2 * grad.size * fsdp_size * size,
    )


def finish_kernel(group, piece, ids_ref, *refs):
    out_ref = refs[group]
    for k in range(group):
        for half in range(refs[k].shape[0] // piece):
            start = pl.multiple_of((half * group + ids_ref[k]) * piece, piece)
            out_ref[pl.ds(start, piece), :] = refs[k][half * piece : (half + 1) * piece, :].astype(F32)


def finish(ids, blocks, piece):
    group = len(blocks)
    rows, width = blocks[0].shape
    if piece % 16:
        order = jnp.take(jnp.stack(blocks), ids, axis=0).reshape(group, rows // piece, piece, width)
        return order.swapaxes(0, 1).reshape(group * rows, width).astype(F32)
    return pallas(
        functools.partial(finish_kernel, group, piece),
        shape((group * rows, width), F32),
        [ids],
        blocks,
        "finish",
        0,
    )


def swap(array, axis, size, distance):
    return lax.ppermute(array, axis, [(i, i ^ distance) for i in range(size)])


def spread(part, size):
    array, distances = part
    return [(swap(array, "ctx", size, k), [k ^ d for d in distances]) for k in range(2, size, 2)]


def widen(parts, size):
    arrays = [array for array, _ in parts]
    whole = jnp.concatenate(arrays, axis=0) if len(arrays) > 1 else arrays[0]
    return swap(whole, "ctx", size, 1), [1 ^ d for _, distances in parts for d in distances]


def after(part, done):
    array, *_ = lax.optimization_barrier((part[0], *[other for other, _ in done]))
    return array, part[1]


def local(ctx_size, fsdp_size, hidden_in, page_tokens, grad_attn, w_qkv):
    hidden, grad_out = hidden_in[0], grad_attn[0]
    rows, depth = hidden.shape
    hd = grad_out.shape[1]
    f, c = lax.axis_index("fsdp"), lax.axis_index("ctx")
    fsdp_ids = f ^ jnp.arange(fsdp_size, dtype=jnp.int32)
    group = min(4, ctx_size)
    group_ids = (c % group) ^ jnp.arange(group, dtype=jnp.int32)

    top = fsdp_size // 2
    weights = {0: w_qkv, top: swap(w_qkv, "fsdp", fsdp_size, top)}
    chunks = list(cut(group_ids, hidden, group, fsdp_size, ctx_size))
    grads = [after((grad_out, [0]), [(chunks[1], 0)])]
    grads += spread(grads[0], ctx_size)
    hidden_parts = {0: chunks[0], **{k: swap(chunks[k], "ctx", ctx_size, k) for k in range(2, group - 1)}}
    weights[top], arrays = lax.optimization_barrier((weights[top], [array for array, _ in grads]))
    grads = [(array, distances) for array, (_, distances) in zip(arrays, grads)]
    grads.append(widen(grads, ctx_size))
    bit = top // 2
    while bit:
        weights.update({k ^ bit: swap(weights[k], "fsdp", fsdp_size, bit) for k in list(weights)})
        bit //= 2
    weights = [weights[k] for k in range(fsdp_size)]

    qk, v = project(fsdp_ids, hidden, weights, (2 * hd, hd))
    qk, late = lax.optimization_barrier((qk, grads[-1][0]))
    grads[-1] = late, grads[-1][1]
    chunks[1], _ = after((chunks[1], 0), [(qk, 0)])
    hidden_parts[1] = swap(chunks[1], "ctx", ctx_size, 1)
    qks = [(qk, [0])]
    qks += spread(qks[0], ctx_size)
    v_pair = [(v, [0]), widen([(v, [0])], ctx_size)]
    pair = jnp.concatenate([array for array, _ in v_pair], axis=0), [0, 1]
    vs = [pair, *spread(after(pair, qks[1:]), ctx_size)]
    qks.append(widen([after(qks[0], [pair, (hidden_parts[2], 0)]), *qks[1:]], ctx_size))
    late, _ = after((chunks[group - 1], 0), vs[1:])
    hidden_parts[group - 1] = swap(late, "ctx", ctx_size, group - 1)
    hidden_parts = [hidden_parts[k] for k in range(group)]
    block = c.reshape(1).astype(jnp.int32)
    grad_near, grad_own = attend(block, page_tokens, [qks, vs, grads], ctx_size, group)
    grad_inputs = hidden_grad(fsdp_ids, grad_own, weights, depth)

    kept, away = weight_grad(group_ids, fsdp_ids, grad_near, hidden_parts)
    bit = 1
    while bit < fsdp_size:
        total = kept + swap(away, "fsdp", fsdp_size, bit).astype(F32)
        bit *= 2
        if bit < fsdp_size:
            kept, away = total[0::2], total[1::2].astype(BF16)
    total = total[0]
    bit = group
    while bit < ctx_size:
        half = total.astype(BF16)
        total = half.astype(F32) + swap(half, "ctx", ctx_size, bit).astype(F32)
        bit *= 2
    total, grad_inputs = lax.optimization_barrier((total.astype(BF16), grad_inputs))
    gathered = [swap(total, "ctx", ctx_size, k) if k else total for k in range(group)]
    grad_weights = finish(group_ids, gathered, depth // (fsdp_size * ctx_size))
    return grad_inputs[None], grad_weights


def solution(mesh):
    in_specs = (P("fsdp", "ctx", None), P("fsdp", None), P("fsdp", "ctx", None), P("fsdp", None))
    out_specs = (P("fsdp", "ctx", None), P("fsdp", None))
    body = functools.partial(local, mesh.shape["ctx"], mesh.shape["fsdp"])
    return jax.shard_map(body, mesh=mesh, in_specs=in_specs, out_specs=out_specs, check_vma=False)
```

```python
import functools
import math

import jax
import jax.numpy as jnp
from jax import lax
from jax.experimental import pallas as pl
from jax.experimental.pallas import tpu as pltpu
from jax.sharding import PartitionSpec as P

F32 = jnp.float32
BF16 = jnp.bfloat16
VMEM = pl.BlockSpec(memory_space=pltpu.VMEM)
SMEM = pl.BlockSpec(memory_space=pltpu.SMEM)
ANY = pl.BlockSpec(memory_space=pltpu.HBM)
MIB = 1024 * 1024


def nt(left, right):
    return lax.dot_general(left, right, (((1,), (1,)), ((), ())), preferred_element_type=F32)


def nn(left, right):
    return jnp.dot(left, right, preferred_element_type=F32)


def tn(left, right):
    return lax.dot_general(left, right, (((0,), (0,)), ((), ())), preferred_element_type=F32)


def pallas(kernel, out_shape, scalars, arrays, name, flops, scratch=(), far=()):
    outs = out_shape if isinstance(out_shape, tuple) else (out_shape,)
    moved = sum(a.size * a.dtype.itemsize for a in (*arrays, *far, *outs))
    held = moved + sum(math.prod(a.shape) * jnp.dtype(a.dtype).itemsize for a in scratch)
    return pl.pallas_call(
        kernel,
        out_shape=out_shape,
        in_specs=[SMEM] * len(scalars) + [VMEM] * len(arrays) + [ANY] * len(far),
        out_specs=jax.tree.map(lambda _: VMEM, out_shape),
        scratch_shapes=[*scratch]
        + [pltpu.VMEM(a.shape, a.dtype) for a in far]
        + [pltpu.SemaphoreType.DMA] * len(far),
        compiler_params=pltpu.CompilerParams(vmem_limit_bytes=min(held + 8 * MIB, 60 * MIB)),
        cost_estimate=pl.CostEstimate(flops=flops, bytes_accessed=moved, transcendentals=0),
        name=name,
    )(*scalars, *arrays, *far)


def shape(dims, dtype=BF16):
    return jax.ShapeDtypeStruct(dims, dtype)


def cut_copies(members, outs, group, piece, ids_ref, hidden_ref, sems):
    copies = []
    for k, out in zip(members, outs):
        for block in range(out.shape[1] // piece):
            start = pl.multiple_of((block * group + ids_ref[k]) * piece, piece)
            source = hidden_ref.at[:, pl.ds(start, piece)]
            target = out.at[:, pl.ds(block * piece, piece)]
            copies.append(pltpu.make_async_copy(source, target, sems.at[len(copies)]))
            copies[len(copies) - 1].start()
    return copies


def cut_kernel(members, group, piece, ids_ref, hidden_ref, *refs):
    for copy in cut_copies(members, refs[: len(members)], group, piece, ids_ref, hidden_ref, refs[len(members)]):
        copy.wait()


def cut_plain(ids, hidden, k, group, piece):
    rows, depth = hidden.shape
    pieces = hidden.reshape(rows, depth // (group * piece), group, piece)
    return lax.dynamic_index_in_dim(pieces, ids[k], 2, keepdims=False).reshape(rows, depth // group)


def cut(ids, hidden, members, group, piece):
    rows, depth = hidden.shape
    if piece % 128:
        return [cut_plain(ids, hidden, k, group, piece) for k in members]
    count = len(members)
    return pl.pallas_call(
        functools.partial(cut_kernel, members, group, piece),
        out_shape=tuple(shape((rows, depth // group)) for _ in members),
        in_specs=[SMEM, ANY],
        out_specs=(VMEM,) * count,
        scratch_shapes=[pltpu.SemaphoreType.DMA((count * depth // (group * piece),))],
        compiler_params=pltpu.CompilerParams(vmem_limit_bytes=8 * MIB),
        cost_estimate=pl.CostEstimate(flops=0, bytes_accessed=hidden.size * count, transcendentals=0),
        name="cut",
    )(ids, hidden)


def fetch(sources, slots):
    count = len(sources)
    copies = [pltpu.make_async_copy(sources[i], slots[i], slots[count + i]) for i in range(count)]
    for copy in copies:
        copy.start()
    return copies


def project_kernel(places, ids_ref, *refs):
    count = len(places)
    slots = refs[len(refs) - 2 * (count + 1) :]
    copies = fetch(refs[: count + 1], slots)
    hidden = slots[count]
    size = sum(slots[i].shape[0] for i in range(count) if places[i][0] == 0)
    copies[count].wait()
    total = None
    for i, (part, first) in enumerate(places):
        rows = slots[i].shape[0]
        start = pl.multiple_of(ids_ref[part] * size + first, rows)
        copies[i].wait()
        term = nn(hidden[:, pl.ds(start, rows)], slots[i][...])
        total = term if total is None else total + term
    first = 0
    for out in refs[count + 1 : len(refs) - 2 * (count + 1)]:
        width = out.shape[1]
        out[...] = total[:, first : first + width].astype(BF16)
        first += width


def project(ids, hidden, weights, widths):
    return pallas(
        functools.partial(project_kernel, [place for _, *place in weights]),
        tuple(shape((hidden.shape[0], width)) for width in widths),
        [ids],
        [],
        "project",
        2 * hidden.size * sum(widths),
        far=[*[array for array, *_ in weights], hidden],
    )


def hidden_kernel(places, ids_ref, grad_ref, *refs):
    count = len(places)
    slots = refs[count + 1 :]
    copies = fetch(refs[:count], slots)
    size = sum(slots[i].shape[0] for i in range(count) if places[i][0] == 0)
    for i, (part, first) in enumerate(places):
        rows = slots[i].shape[0]
        start = pl.multiple_of(ids_ref[part] * size + first, rows)
        copies[i].wait()
        refs[count][:, pl.ds(start, rows)] = nt(grad_ref[...], slots[i][...]).astype(BF16)


def hidden_grad(ids, grad, weights, depth):
    return pallas(
        functools.partial(hidden_kernel, [place for _, *place in weights]),
        shape((grad.shape[0], depth)),
        [ids],
        [grad],
        "hidden_grad",
        2 * grad.size * depth,
        far=[array for array, *_ in weights],
    )


def attend_kernel(layouts, group, rows, bq, bk, block_ref, pages_ref, *refs):
    count = sum(len(layout) for layout in layouts)
    parts, (grad_ref, own_ref) = refs[:count], refs[count : count + 2]
    q_ref, k_ref, v_ref, do_ref, s_ref, dp_ref, dk_ref, dv_ref, kt_ref, m_ref = refs[count + 2 :]
    seq, hd = do_ref.shape
    near = rows * group
    block = block_ref[0]
    scale = hd**-0.5
    scale2 = scale * math.log2(math.e)
    at = 0
    for layout, targets in zip(layouts, ((q_ref, k_ref), (v_ref,), (do_ref,))):
        for distances in layout:
            for number, distance in enumerate(distances):
                here = pl.ds(pl.multiple_of((block ^ distance) * rows, rows), rows)
                for column, target in enumerate(targets):
                    target[here, :] = parts[at][number * rows : (number + 1) * rows, column * hd : (column + 1) * hd]
            at += 1
    dk_ref[...] = jnp.zeros_like(dk_ref)
    dv_ref[...] = jnp.zeros_like(dv_ref)
    kt_ref[...] = k_ref[...].T
    ends, end = [], jnp.int32(0)
    for page in range(pages_ref.shape[1]):
        end = end + pages_ref[0, page]
        ends.append(end)
    low = lax.div(block, group) * near
    near_first, near_last = lax.div(low, bk), lax.div(low, bk) + near // bk

    def limit_of(pos):
        limit = jnp.full_like(pos, seq)
        for page_end in ends:
            limit = jnp.minimum(limit, jnp.where(page_end > pos, page_end, seq))
        return limit

    @pl.loop(0, seq // bq)
    def _(i):
        q0 = pl.multiple_of(i * bq, bq)
        limits = limit_of(q0 + lax.broadcasted_iota(jnp.int32, (1, bq), 1))
        count = lax.div(limit_of(q0 + (bq - 1)) + (bk - 1), bk)
        first, last = jnp.minimum(near_first, count), jnp.minimum(near_last, count)
        is_near = (q0 >= low) & (q0 < low + near)

        @pl.when(is_near | (first < last))
        def _():
            q = q_ref[pl.ds(q0, bq), :]
            do = do_ref[pl.ds(q0, bq), :]
            qt, dot_t = q.T, do.T

            def scores(masked, j, carry):
                row_max, total, dot = carry
                k0 = pl.multiple_of(j * bk, bk)
                s = nn(k_ref[pl.ds(k0, bk), :], qt) * scale2
                if masked:
                    key = k0 + lax.broadcasted_iota(jnp.int32, (bk, 1), 0)
                    s = jnp.where(key < limits, s, -1e30)
                high = jnp.maximum(row_max, jnp.max(s, axis=0, keepdims=True))
                p = jnp.exp2(s - high)
                dp = nn(v_ref[pl.ds(k0, bk), :], dot_t)
                s_ref[pl.ds(k0, bk), :] = p
                dp_ref[pl.ds(k0, bk), :] = dp
                m_ref[j] = high
                fade = jnp.exp2(row_max - high)
                total = total * fade + jnp.sum(p, axis=0, keepdims=True)
                dot = dot * fade + jnp.sum(p * dp, axis=0, keepdims=True)
                return high, total, dot

            zero = jnp.zeros((1, bq), F32)
            carry = (jnp.full((1, bq), -3e38, F32), zero, zero)
            full = jnp.minimum(lax.div(q0, bk), count)
            carry = lax.fori_loop(0, full, functools.partial(scores, False), carry)
            row_max, total, dot = lax.fori_loop(full, count, functools.partial(scores, True), carry)
            inv = 1.0 / total
            dot = dot * inv

            def dscore(j):
                k0 = pl.multiple_of(j * bk, bk)
                share = jnp.exp2(m_ref[j] - row_max) * inv
                gain = share * scale
                p = s_ref[pl.ds(k0, bk), :]
                return k0, p * share, (p * (dp_ref[pl.ds(k0, bk), :] * gain - dot * gain)).astype(BF16)

            def key_grads(j, carry):
                k0, p, ds = dscore(j)
                dv_ref[pl.ds(k0 - low, bk), :] += nn(p.astype(BF16), do)
                dk_ref[pl.ds(k0 - low, bk), :] += nn(ds, q)
                return carry

            def query_grads(j, dqt):
                k0, _, ds = dscore(j)
                return dqt + nn(kt_ref[:, pl.ds(k0, bk)], ds)

            def all_grads(j, dqt):
                k0, p, ds = dscore(j)
                dv_ref[pl.ds(k0 - low, bk), :] += nn(p.astype(BF16), do)
                dk_ref[pl.ds(k0 - low, bk), :] += nn(ds, q)
                return dqt + nn(kt_ref[:, pl.ds(k0, bk)], ds)

            @pl.when(is_near)
            def _():
                dqt = lax.fori_loop(0, first, query_grads, jnp.zeros((hd, bq), F32))
                dqt = lax.fori_loop(first, last, all_grads, dqt)
                dqt = lax.fori_loop(last, count, query_grads, dqt)
                grad_ref[pl.ds(pl.multiple_of(q0 - low, bq), bq), :hd] = dqt.T.astype(BF16)

            @pl.when(jnp.logical_not(is_near))
            def _():
                lax.fori_loop(first, last, key_grads, 0)

    grad_ref[:, hd : 2 * hd] = dk_ref[...].astype(BF16)
    grad_ref[:, 2 * hd :] = dv_ref[...].astype(BF16)
    own = pl.multiple_of(lax.rem(block, group) * rows, rows)
    own_ref[...] = grad_ref[pl.ds(own, rows), :]


def attend(block, pages, sets, blocks, group):
    rows = sets[0][0][0].shape[0] // len(sets[0][0][1])
    hd = sets[1][0][0].shape[1]
    seq, near = rows * blocks, rows * group
    bq, bk = (near, 2 * rows) if seq <= 4096 else (rows, rows)
    layouts = [[distances for _, distances in parts] for parts in sets]
    return pallas(
        functools.partial(attend_kernel, layouts, group, rows, bq, bk),
        (shape((near, 3 * hd)), shape((rows, 3 * hd))),
        [block, pages],
        [array for parts in sets for array, _ in parts],
        "attend",
        10 * seq * seq * hd,
        [pltpu.VMEM((seq, hd), BF16)] * 4
        + [pltpu.VMEM((seq, bq), F32)] * 2
        + [pltpu.VMEM((near, hd), F32)] * 2
        + [pltpu.VMEM((hd, seq), BF16), pltpu.VMEM((seq // bk, 1, bq), F32)],
    )


def weight_kernel(group, piece, ids_ref, fsdp_ref, grad_ref, hidden_ref, *refs):
    parts, (kept_ref, away_ref, own_ref, sems) = refs[: group - 1], refs[group - 1 :]
    copies = cut_copies([0], [own_ref], group, piece, ids_ref, hidden_ref, sems)
    rows, width = own_ref.shape
    fsdp_size = 2 * kept_ref.shape[0]
    size = width // fsdp_size
    for copy in copies:
        copy.wait()
    for j in range(fsdp_size):
        columns = pl.ds(pl.multiple_of(fsdp_ref[j] * size, size), size)
        total = None
        for k, part in enumerate((own_ref, *parts)):
            here = pl.ds(pl.multiple_of(ids_ref[k] * rows, rows), rows)
            term = tn(part[:, columns], grad_ref[here, :])
            total = term if total is None else total + term
        out = away_ref if j % 2 else kept_ref
        out[j // 2] = total.astype(out.dtype)


def weight_grad(ids, fsdp_ids, grad, hidden, parts, piece):
    group, fsdp_size, width = len(parts) + 1, fsdp_ids.shape[0], grad.shape[1]
    rows, columns = parts[0].shape
    size = columns // fsdp_size
    half = (fsdp_size // 2, size, width)
    if piece % 128:
        parts = [cut_plain(ids, hidden, 0, group, piece), *parts]
        total = sum(tn(parts[k], lax.dynamic_slice_in_dim(grad, ids[k] * rows, rows, 0)) for k in range(group))
        both = jnp.take(total.reshape(fsdp_size, size, width), fsdp_ids, axis=0)
        both = both.reshape(fsdp_size // 2, 2, size, width)
        return both[:, 0], both[:, 1].astype(BF16)
    return pl.pallas_call(
        functools.partial(weight_kernel, group, piece),
        out_shape=(shape(half, F32), shape(half)),
        in_specs=[SMEM, SMEM, VMEM, ANY] + [VMEM] * (group - 1),
        out_specs=(VMEM, VMEM),
        scratch_shapes=[pltpu.VMEM((rows, columns), BF16), pltpu.SemaphoreType.DMA((columns // piece,))],
        compiler_params=pltpu.CompilerParams(vmem_limit_bytes=20 * MIB),
        cost_estimate=pl.CostEstimate(flops=2 * grad.size * columns, bytes_accessed=8 * MIB, transcendentals=0),
        name="weight_grad",
    )(ids, fsdp_ids, grad, hidden, *parts)


def finish_kernel(group, piece, ids_ref, *refs):
    out_ref = refs[group]
    for k in range(group):
        for half in range(refs[k].shape[0] // piece):
            start = pl.multiple_of((half * group + ids_ref[k]) * piece, piece)
            out_ref[pl.ds(start, piece), :] = refs[k][half * piece : (half + 1) * piece, :].astype(F32)


def finish(ids, blocks, piece):
    group = len(blocks)
    rows, width = blocks[0].shape
    if piece % 16:
        order = jnp.take(jnp.stack(blocks), ids, axis=0).reshape(group, rows // piece, piece, width)
        return order.swapaxes(0, 1).reshape(group * rows, width).astype(F32)
    return pallas(
        functools.partial(finish_kernel, group, piece),
        shape((group * rows, width), F32),
        [ids],
        blocks,
        "finish",
        0,
    )


def swap(array, axis, size, distance):
    return lax.ppermute(array, axis, [(i, i ^ distance) for i in range(size)])


def spread(part, size):
    array, distances = part
    return [(swap(array, "ctx", size, k), [k ^ d for d in distances]) for k in range(2, size, 2)]


def widen(parts, size):
    arrays = [array for array, _ in parts]
    whole = jnp.concatenate(arrays, axis=0) if len(arrays) > 1 else arrays[0]
    return swap(whole, "ctx", size, 1), [1 ^ d for _, distances in parts for d in distances]


def after(part, done):
    array, *_ = lax.optimization_barrier((part[0], *[other for other, _ in done]))
    return array, part[1]


def local(ctx_size, fsdp_size, hidden_in, page_tokens, grad_attn, w_qkv):
    hidden, grad_out = hidden_in[0], grad_attn[0]
    rows, depth = hidden.shape
    hd = grad_out.shape[1]
    f, c = lax.axis_index("fsdp"), lax.axis_index("ctx")
    fsdp_ids = f ^ jnp.arange(fsdp_size, dtype=jnp.int32)
    group = min(4, ctx_size)
    group_ids = (c % group) ^ jnp.arange(group, dtype=jnp.int32)

    piece = depth // (fsdp_size * ctx_size)
    top = fsdp_size // 2
    weights = {0: [w_qkv], top: [swap(w_qkv, "fsdp", fsdp_size, top)]}
    chunks = dict(zip((1, 2), cut(group_ids, hidden, (1, 2), group, piece)))
    grads = [(grad_out, [0])]
    grads += spread(grads[0], ctx_size)
    moved = {k: swap(chunks[k], "ctx", ctx_size, k) for k in (1, 2)}
    arrays, _ = lax.optimization_barrier(([array for array, _ in grads], chunks))
    grads = [(array, distances) for array, (_, distances) in zip(arrays, grads)]
    whole = jnp.concatenate([array for array, _ in grads], axis=0)
    array, distances = widen([(whole, [d for _, distances in grads for d in distances])], ctx_size)
    weights[top], array = lax.optimization_barrier((weights[top], array))
    grads.append((array, distances))
    bit = top // 2
    while bit:
        for k in list(weights):
            halves = weights[k]
            weights[k ^ bit] = [swap(half, "fsdp", fsdp_size, bit) for half in halves]
        bit //= 2
    size = w_qkv.shape[0]
    weights = [
        (array, k, number * (size // len(weights[k]))) for k in range(fsdp_size) for number, array in enumerate(weights[k])
    ]

    qk, v = project(fsdp_ids, hidden, weights, (2 * hd, hd))
    qks = [(qk, [0])]
    qks += spread(qks[0], ctx_size)
    v_pair = [(v, [0]), widen([after((v, [0]), [(moved[1], 0)])], ctx_size)]
    pair = jnp.concatenate([array for array, _ in v_pair], axis=0), [0, 1]
    vs = [pair, *spread(after(pair, qks[1:]), ctx_size)]
    qks.append(widen([after(qks[0], [pair, (moved[1], 0), (moved[2], 0)]), *qks[1:]], ctx_size))
    (late,) = cut(group_ids, after((hidden, 0), [(qk, 0)])[0], (3,), group, piece)
    moved[3] = swap(after((late, 0), vs[1:])[0], "ctx", ctx_size, 3)
    block = c.reshape(1).astype(jnp.int32)
    grad_near, grad_own = attend(block, page_tokens, [qks, vs, grads], ctx_size, group)
    grad_inputs = hidden_grad(fsdp_ids, grad_own, weights, depth)

    kept, away = weight_grad(group_ids, fsdp_ids, grad_near, hidden, [moved[k] for k in (1, 2, 3)], piece)
    bit = 1
    while bit < fsdp_size:
        total = kept + swap(away, "fsdp", fsdp_size, bit).astype(F32)
        bit *= 2
        if bit < fsdp_size:
            kept, away = total[0::2], total[1::2].astype(BF16)
    total = total[0]
    bit = group
    while bit < ctx_size:
        half = total.astype(BF16)
        total = half.astype(F32) + swap(half, "ctx", ctx_size, bit).astype(F32)
        bit *= 2
    total, grad_inputs = lax.optimization_barrier((total.astype(BF16), grad_inputs))
    gathered = [swap(total, "ctx", ctx_size, k) if k else total for k in range(group)]
    grad_weights = finish(group_ids, gathered, depth // (fsdp_size * ctx_size))
    return grad_inputs[None], grad_weights


def solution(mesh):
    in_specs = (P("fsdp", "ctx", None), P("fsdp", None), P("fsdp", "ctx", None), P("fsdp", None))
    out_specs = (P("fsdp", "ctx", None), P("fsdp", None))
    body = functools.partial(local, mesh.shape["ctx"], mesh.shape["fsdp"])
    return jax.shard_map(body, mesh=mesh, in_specs=in_specs, out_specs=out_specs, check_vma=False)
```

```python
import functools
import math

import jax
import jax.numpy as jnp
from jax import lax
from jax.experimental import pallas as pl
from jax.experimental.pallas import tpu as pltpu
from jax.sharding import PartitionSpec as P

F32 = jnp.float32
BF16 = jnp.bfloat16
VMEM = pl.BlockSpec(memory_space=pltpu.VMEM)
SMEM = pl.BlockSpec(memory_space=pltpu.SMEM)
ANY = pl.BlockSpec(memory_space=pltpu.HBM)
MIB = 1024 * 1024


def nt(left, right):
    return lax.dot_general(left, right, (((1,), (1,)), ((), ())), preferred_element_type=F32)


def nn(left, right):
    return jnp.dot(left, right, preferred_element_type=F32)


def tn(left, right):
    return lax.dot_general(left, right, (((0,), (0,)), ((), ())), preferred_element_type=F32)


def pallas(kernel, out_shape, scalars, arrays, name, flops, scratch=(), far=()):
    outs = out_shape if isinstance(out_shape, tuple) else (out_shape,)
    moved = sum(a.size * a.dtype.itemsize for a in (*arrays, *far, *outs))
    held = moved + sum(math.prod(a.shape) * jnp.dtype(a.dtype).itemsize for a in scratch)
    return pl.pallas_call(
        kernel,
        out_shape=out_shape,
        in_specs=[SMEM] * len(scalars) + [VMEM] * len(arrays) + [ANY] * len(far),
        out_specs=jax.tree.map(lambda _: VMEM, out_shape),
        scratch_shapes=[*scratch]
        + [pltpu.VMEM(a.shape, a.dtype) for a in far]
        + [pltpu.SemaphoreType.DMA] * len(far),
        compiler_params=pltpu.CompilerParams(vmem_limit_bytes=min(held + 8 * MIB, 60 * MIB)),
        cost_estimate=pl.CostEstimate(flops=flops, bytes_accessed=moved, transcendentals=0),
        name=name,
    )(*scalars, *arrays, *far)


def shape(dims, dtype=BF16):
    return jax.ShapeDtypeStruct(dims, dtype)


def cut_copies(members, outs, group, piece, ids_ref, hidden_ref, sems):
    copies = []
    for k, out in zip(members, outs):
        for block in range(out.shape[1] // piece):
            start = pl.multiple_of((block * group + ids_ref[k]) * piece, piece)
            source = hidden_ref.at[:, pl.ds(start, piece)]
            target = out.at[:, pl.ds(block * piece, piece)]
            copies.append(pltpu.make_async_copy(source, target, sems.at[len(copies)]))
            copies[len(copies) - 1].start()
    return copies


def cut_kernel(members, group, piece, ids_ref, hidden_ref, *refs):
    for copy in cut_copies(members, refs[: len(members)], group, piece, ids_ref, hidden_ref, refs[len(members)]):
        copy.wait()


def cut_plain(ids, hidden, k, group, piece):
    rows, depth = hidden.shape
    pieces = hidden.reshape(rows, depth // (group * piece), group, piece)
    return lax.dynamic_index_in_dim(pieces, ids[k], 2, keepdims=False).reshape(rows, depth // group)


def cut(ids, hidden, members, group, piece):
    rows, depth = hidden.shape
    if piece % 128:
        return [cut_plain(ids, hidden, k, group, piece) for k in members]
    count = len(members)
    return pl.pallas_call(
        functools.partial(cut_kernel, members, group, piece),
        out_shape=tuple(shape((rows, depth // group)) for _ in members),
        in_specs=[SMEM, ANY],
        out_specs=(VMEM,) * count,
        scratch_shapes=[pltpu.SemaphoreType.DMA((count * depth // (group * piece),))],
        compiler_params=pltpu.CompilerParams(vmem_limit_bytes=8 * MIB),
        cost_estimate=pl.CostEstimate(flops=0, bytes_accessed=hidden.size * count, transcendentals=0),
        name="cut",
    )(ids, hidden)


def fetch(sources, slots):
    count = len(sources)
    copies = [pltpu.make_async_copy(sources[i], slots[i], slots[count + i]) for i in range(count)]
    for copy in copies:
        copy.start()
    return copies


def project_kernel(places, ids_ref, *refs):
    count = len(places)
    slots = refs[len(refs) - 2 * (count + 1) :]
    copies = fetch(refs[: count + 1], slots)
    hidden = slots[count]
    size = sum(slots[i].shape[0] for i in range(count) if places[i][0] == 0)
    copies[count].wait()
    total = None
    for i, (part, first) in enumerate(places):
        rows = slots[i].shape[0]
        start = pl.multiple_of(ids_ref[part] * size + first, rows)
        copies[i].wait()
        term = nn(hidden[:, pl.ds(start, rows)], slots[i][...])
        total = term if total is None else total + term
    first = 0
    for out in refs[count + 1 : len(refs) - 2 * (count + 1)]:
        width = out.shape[1]
        out[...] = total[:, first : first + width].astype(BF16)
        first += width


def project(ids, hidden, weights, widths):
    return pallas(
        functools.partial(project_kernel, [place for _, *place in weights]),
        tuple(shape((hidden.shape[0], width)) for width in widths),
        [ids],
        [],
        "project",
        2 * hidden.size * sum(widths),
        far=[*[array for array, *_ in weights], hidden],
    )


def hidden_kernel(places, ids_ref, grad_ref, *refs):
    count = len(places)
    slots = refs[count + 1 :]
    copies = fetch(refs[:count], slots)
    size = sum(slots[i].shape[0] for i in range(count) if places[i][0] == 0)
    for i, (part, first) in enumerate(places):
        rows = slots[i].shape[0]
        start = pl.multiple_of(ids_ref[part] * size + first, rows)
        copies[i].wait()
        refs[count][:, pl.ds(start, rows)] = nt(grad_ref[...], slots[i][...]).astype(BF16)


def hidden_grad(ids, grad, weights, depth):
    return pallas(
        functools.partial(hidden_kernel, [place for _, *place in weights]),
        shape((grad.shape[0], depth)),
        [ids],
        [grad],
        "hidden_grad",
        2 * grad.size * depth,
        far=[array for array, *_ in weights],
    )


def attend_kernel(layouts, group, rows, bq, bk, block_ref, pages_ref, *refs):
    count = sum(len(layout) for layout in layouts)
    parts, (grad_ref, own_ref) = refs[:count], refs[count : count + 2]
    q_ref, k_ref, v_ref, do_ref, s_ref, dp_ref, dk_ref, dv_ref, kt_ref, m_ref = refs[count + 2 :]
    seq, hd = do_ref.shape
    near = rows * group
    block = block_ref[0]
    scale = hd**-0.5
    scale2 = scale * math.log2(math.e)
    at = 0
    for layout, targets in zip(layouts, ((q_ref, k_ref), (v_ref,), (do_ref,))):
        for distances in layout:
            for number, distance in enumerate(distances):
                here = pl.ds(pl.multiple_of((block ^ distance) * rows, rows), rows)
                for column, target in enumerate(targets):
                    target[here, :] = parts[at][number * rows : (number + 1) * rows, column * hd : (column + 1) * hd]
            at += 1
    dk_ref[...] = jnp.zeros_like(dk_ref)
    dv_ref[...] = jnp.zeros_like(dv_ref)
    kt_ref[...] = k_ref[...].T
    ends, end = [], jnp.int32(0)
    for page in range(pages_ref.shape[1]):
        end = end + pages_ref[0, page]
        ends.append(end)
    low = lax.div(block, group) * near
    near_first, near_last = lax.div(low, bk), lax.div(low, bk) + near // bk

    def limit_of(pos):
        limit = jnp.full_like(pos, seq)
        for page_end in ends:
            limit = jnp.minimum(limit, jnp.where(page_end > pos, page_end, seq))
        return limit

    @pl.loop(0, seq // bq)
    def _(i):
        q0 = pl.multiple_of(i * bq, bq)
        limits = limit_of(q0 + lax.broadcasted_iota(jnp.int32, (1, bq), 1))
        count = lax.div(limit_of(q0 + (bq - 1)) + (bk - 1), bk)
        first, last = jnp.minimum(near_first, count), jnp.minimum(near_last, count)
        is_near = (q0 >= low) & (q0 < low + near)

        @pl.when(is_near | (first < last))
        def _():
            q = q_ref[pl.ds(q0, bq), :]
            do = do_ref[pl.ds(q0, bq), :]
            qt, dot_t = q.T, do.T

            def scores(masked, j, carry):
                row_max, total, dot = carry
                k0 = pl.multiple_of(j * bk, bk)
                s = nn(k_ref[pl.ds(k0, bk), :], qt) * scale2
                if masked:
                    key = k0 + lax.broadcasted_iota(jnp.int32, (bk, 1), 0)
                    s = jnp.where(key < limits, s, -1e30)
                high = jnp.maximum(row_max, jnp.max(s, axis=0, keepdims=True))
                p = jnp.exp2(s - high)
                dp = nn(v_ref[pl.ds(k0, bk), :], dot_t)
                s_ref[pl.ds(k0, bk), :] = p
                dp_ref[pl.ds(k0, bk), :] = dp
                m_ref[j] = high
                fade = jnp.exp2(row_max - high)
                total = total * fade + jnp.sum(p, axis=0, keepdims=True)
                dot = dot * fade + jnp.sum(p * dp, axis=0, keepdims=True)
                return high, total, dot

            zero = jnp.zeros((1, bq), F32)
            carry = (jnp.full((1, bq), -3e38, F32), zero, zero)
            full = jnp.minimum(lax.div(q0, bk), count)
            carry = lax.fori_loop(0, full, functools.partial(scores, False), carry)
            row_max, total, dot = lax.fori_loop(full, count, functools.partial(scores, True), carry)
            inv = 1.0 / total
            dot = dot * inv

            def dscore(j):
                k0 = pl.multiple_of(j * bk, bk)
                share = jnp.exp2(m_ref[j] - row_max) * inv
                gain = share * scale
                p = s_ref[pl.ds(k0, bk), :]
                return k0, p * share, (p * (dp_ref[pl.ds(k0, bk), :] * gain - dot * gain)).astype(BF16)

            def key_grads(j, carry):
                k0, p, ds = dscore(j)
                dv_ref[pl.ds(k0 - low, bk), :] += nn(p.astype(BF16), do)
                dk_ref[pl.ds(k0 - low, bk), :] += nn(ds, q)
                return carry

            def query_grads(j, dqt):
                k0, _, ds = dscore(j)
                return dqt + nn(kt_ref[:, pl.ds(k0, bk)], ds)

            def all_grads(j, dqt):
                k0, p, ds = dscore(j)
                dv_ref[pl.ds(k0 - low, bk), :] += nn(p.astype(BF16), do)
                dk_ref[pl.ds(k0 - low, bk), :] += nn(ds, q)
                return dqt + nn(kt_ref[:, pl.ds(k0, bk)], ds)

            @pl.when(is_near)
            def _():
                dqt = lax.fori_loop(0, first, query_grads, jnp.zeros((hd, bq), F32))
                dqt = lax.fori_loop(first, last, all_grads, dqt)
                dqt = lax.fori_loop(last, count, query_grads, dqt)
                grad_ref[pl.ds(pl.multiple_of(q0 - low, bq), bq), :hd] = dqt.T.astype(BF16)

            @pl.when(jnp.logical_not(is_near))
            def _():
                lax.fori_loop(first, last, key_grads, 0)

    grad_ref[:, hd : 2 * hd] = dk_ref[...].astype(BF16)
    grad_ref[:, 2 * hd :] = dv_ref[...].astype(BF16)
    own = pl.multiple_of(lax.rem(block, group) * rows, rows)
    own_ref[...] = grad_ref[pl.ds(own, rows), :]


def attend(block, pages, sets, blocks, group):
    rows = sets[0][0][0].shape[0] // len(sets[0][0][1])
    hd = sets[1][0][0].shape[1]
    seq, near = rows * blocks, rows * group
    bq, bk = (near, 2 * rows) if seq <= 4096 else (rows, rows)
    layouts = [[distances for _, distances in parts] for parts in sets]
    return pallas(
        functools.partial(attend_kernel, layouts, group, rows, bq, bk),
        (shape((near, 3 * hd)), shape((rows, 3 * hd))),
        [block, pages],
        [array for parts in sets for array, _ in parts],
        "attend",
        10 * seq * seq * hd,
        [pltpu.VMEM((seq, hd), BF16)] * 4
        + [pltpu.VMEM((seq, bq), F32)] * 2
        + [pltpu.VMEM((near, hd), F32)] * 2
        + [pltpu.VMEM((hd, seq), BF16), pltpu.VMEM((seq // bk, 1, bq), F32)],
    )


def weight_kernel(group, piece, ids_ref, fsdp_ref, grad_ref, hidden_ref, *refs):
    parts, (kept_ref, away_ref, own_ref, sems) = refs[: group - 1], refs[group - 1 :]
    copies = cut_copies([0], [own_ref], group, piece, ids_ref, hidden_ref, sems)
    rows, width = own_ref.shape
    fsdp_size = 2 * kept_ref.shape[0]
    size = width // fsdp_size
    for copy in copies:
        copy.wait()
    for j in range(fsdp_size):
        columns = pl.ds(pl.multiple_of(fsdp_ref[j] * size, size), size)
        total = None
        for k, part in enumerate((own_ref, *parts)):
            here = pl.ds(pl.multiple_of(ids_ref[k] * rows, rows), rows)
            term = tn(part[:, columns], grad_ref[here, :])
            total = term if total is None else total + term
        out = away_ref if j % 2 else kept_ref
        out[j // 2] = total.astype(out.dtype)


def weight_grad(ids, fsdp_ids, grad, hidden, parts, piece):
    group, fsdp_size, width = len(parts) + 1, fsdp_ids.shape[0], grad.shape[1]
    rows, columns = parts[0].shape
    size = columns // fsdp_size
    half = (fsdp_size // 2, size, width)
    if piece % 128:
        parts = [cut_plain(ids, hidden, 0, group, piece), *parts]
        total = sum(tn(parts[k], lax.dynamic_slice_in_dim(grad, ids[k] * rows, rows, 0)) for k in range(group))
        both = jnp.take(total.reshape(fsdp_size, size, width), fsdp_ids, axis=0)
        both = both.reshape(fsdp_size // 2, 2, size, width)
        return both[:, 0], both[:, 1].astype(BF16)
    return pl.pallas_call(
        functools.partial(weight_kernel, group, piece),
        out_shape=(shape(half, F32), shape(half)),
        in_specs=[SMEM, SMEM, VMEM, ANY] + [VMEM] * (group - 1),
        out_specs=(VMEM, VMEM),
        scratch_shapes=[pltpu.VMEM((rows, columns), BF16), pltpu.SemaphoreType.DMA((columns // piece,))],
        compiler_params=pltpu.CompilerParams(vmem_limit_bytes=20 * MIB),
        cost_estimate=pl.CostEstimate(flops=2 * grad.size * columns, bytes_accessed=8 * MIB, transcendentals=0),
        name="weight_grad",
    )(ids, fsdp_ids, grad, hidden, *parts)


def finish_kernel(group, piece, ids_ref, *refs):
    out_ref = refs[len(refs) - 1]
    for number, block in enumerate(refs[: len(refs) - 1]):
        count = block.shape[0] // piece
        for i in range(count):
            place = (number // group * count + i) * group + ids_ref[number % group]
            start = pl.multiple_of(place * piece, piece)
            out_ref[pl.ds(start, piece), :] = block[i * piece : (i + 1) * piece, :].astype(F32)


def finish(ids, blocks, group, piece):
    rows, width = blocks[0].shape
    if piece % 16:
        order = jnp.stack(blocks).reshape(-1, group, rows // piece, piece, width)
        order = jnp.take(order, ids, axis=1).swapaxes(1, 2)
        return order.reshape(len(blocks) * rows, width).astype(F32)
    return pallas(
        functools.partial(finish_kernel, group, piece),
        shape((len(blocks) * rows, width), F32),
        [ids],
        blocks,
        "finish",
        0,
    )


def swap(array, axis, size, distance):
    return lax.ppermute(array, axis, [(i, i ^ distance) for i in range(size)])


def spread(part, size):
    array, distances = part
    return [(swap(array, "ctx", size, k), [k ^ d for d in distances]) for k in range(2, size, 2)]


def widen(parts, size):
    arrays = [array for array, _ in parts]
    whole = jnp.concatenate(arrays, axis=0) if len(arrays) > 1 else arrays[0]
    return swap(whole, "ctx", size, 1), [1 ^ d for _, distances in parts for d in distances]


def after(part, done):
    array, *_ = lax.optimization_barrier((part[0], *[other for other, _ in done]))
    return array, part[1]


def local(ctx_size, fsdp_size, hidden_in, page_tokens, grad_attn, w_qkv):
    hidden, grad_out = hidden_in[0], grad_attn[0]
    rows, depth = hidden.shape
    hd = grad_out.shape[1]
    f, c = lax.axis_index("fsdp"), lax.axis_index("ctx")
    fsdp_ids = f ^ jnp.arange(fsdp_size, dtype=jnp.int32)
    group = min(4, ctx_size)
    group_ids = (c % group) ^ jnp.arange(group, dtype=jnp.int32)

    piece = depth // (fsdp_size * ctx_size)
    top = fsdp_size // 2
    weights = {0: [w_qkv], top: [swap(w_qkv, "fsdp", fsdp_size, top)]}
    chunks = dict(zip((1, 2), cut(group_ids, hidden, (1, 2), group, piece)))
    grads = [(grad_out, [0])]
    grads += spread(grads[0], ctx_size)
    moved = {k: swap(chunks[k], "ctx", ctx_size, k) for k in (1, 2)}
    arrays, _ = lax.optimization_barrier(([array for array, _ in grads], chunks))
    grads = [(array, distances) for array, (_, distances) in zip(arrays, grads)]
    whole = jnp.concatenate([array for array, _ in grads], axis=0)
    array, distances = widen([(whole, [d for _, distances in grads for d in distances])], ctx_size)
    weights[top], array = lax.optimization_barrier((weights[top], array))
    grads.append((array, distances))
    bit = top // 2
    while bit:
        for k in list(weights):
            halves = weights[k]
            weights[k ^ bit] = [swap(half, "fsdp", fsdp_size, bit) for half in halves]
        bit //= 2
    size = w_qkv.shape[0]
    weights = [
        (array, k, number * (size // len(weights[k]))) for k in range(fsdp_size) for number, array in enumerate(weights[k])
    ]

    qk, v = project(fsdp_ids, hidden, weights, (2 * hd, hd))
    qks = [(qk, [0])]
    qks += spread(qks[0], ctx_size)
    v_pair = [(v, [0]), widen([after((v, [0]), [(moved[1], 0)])], ctx_size)]
    pair = jnp.concatenate([array for array, _ in v_pair], axis=0), [0, 1]
    vs = [pair, *spread(after(pair, qks[1:]), ctx_size)]
    qks.append(widen([after(qks[0], [pair, (moved[1], 0), (moved[2], 0)]), *qks[1:]], ctx_size))
    (late,) = cut(group_ids, after((hidden, 0), [(qk, 0)])[0], (3,), group, piece)
    moved[3] = swap(after((late, 0), vs[1:])[0], "ctx", ctx_size, 3)
    block = c.reshape(1).astype(jnp.int32)
    grad_near, grad_own = attend(block, page_tokens, [qks, vs, grads], ctx_size, group)
    kept, away = weight_grad(group_ids, fsdp_ids, grad_near, hidden, [moved[k] for k in (1, 2, 3)], piece)
    bit = 1
    while bit < top:
        total = kept + swap(away, "fsdp", fsdp_size, bit).astype(F32)
        bit *= 2
        kept, away = total[0::2], total[1::2].astype(BF16)
    half = kept.shape[1] // 2
    first = swap(away[0, :half], "fsdp", fsdp_size, top)
    second, first = lax.optimization_barrier((away[0, half:], first))
    second = swap(second, "fsdp", fsdp_size, top)
    totals = [kept[0, :half] + first.astype(F32)]
    rest, total = lax.optimization_barrier((kept[0, half:], totals[0].astype(BF16)))
    grad_own, total = lax.optimization_barrier((grad_own, total))
    grad_inputs = hidden_grad(fsdp_ids, grad_own, weights, depth)
    second, grad_inputs = lax.optimization_barrier((second, grad_inputs))
    totals = [total, rest + second.astype(F32)]
    bit = group
    while bit < ctx_size:
        sent = [total.astype(BF16) for total in totals]
        totals = [own.astype(F32) + swap(own, "ctx", ctx_size, bit).astype(F32) for own in sent]
        bit *= 2
    totals = [total.astype(BF16) for total in totals]
    gathered = [swap(total, "ctx", ctx_size, k) if k else total for total in totals for k in range(group)]
    grad_weights = finish(group_ids, gathered, group, piece)
    return grad_inputs[None], grad_weights


def solution(mesh):
    in_specs = (P("fsdp", "ctx", None), P("fsdp", None), P("fsdp", "ctx", None), P("fsdp", None))
    out_specs = (P("fsdp", "ctx", None), P("fsdp", None))
    body = functools.partial(local, mesh.shape["ctx"], mesh.shape["fsdp"])
    return jax.shard_map(body, mesh=mesh, in_specs=in_specs, out_specs=out_specs, check_vma=False)
```

```python
import functools
import math

import jax
import jax.numpy as jnp
from jax import lax
from jax.experimental import pallas as pl
from jax.experimental.pallas import tpu as pltpu
from jax.sharding import PartitionSpec as P

F32 = jnp.float32
BF16 = jnp.bfloat16
VMEM = pl.BlockSpec(memory_space=pltpu.VMEM)
SMEM = pl.BlockSpec(memory_space=pltpu.SMEM)
ANY = pl.BlockSpec(memory_space=pltpu.HBM)
MIB = 1024 * 1024


def nt(left, right):
    return lax.dot_general(left, right, (((1,), (1,)), ((), ())), preferred_element_type=F32)


def nn(left, right):
    return jnp.dot(left, right, preferred_element_type=F32)


def tn(left, right):
    return lax.dot_general(left, right, (((0,), (0,)), ((), ())), preferred_element_type=F32)


def pallas(kernel, out_shape, scalars, arrays, name, flops, scratch=(), far=()):
    outs = out_shape if isinstance(out_shape, tuple) else (out_shape,)
    moved = sum(a.size * a.dtype.itemsize for a in (*arrays, *far, *outs))
    held = moved + sum(math.prod(a.shape) * jnp.dtype(a.dtype).itemsize for a in scratch)
    return pl.pallas_call(
        kernel,
        out_shape=out_shape,
        in_specs=[SMEM] * len(scalars) + [VMEM] * len(arrays) + [ANY] * len(far),
        out_specs=jax.tree.map(lambda _: VMEM, out_shape),
        scratch_shapes=[*scratch]
        + [pltpu.VMEM(a.shape, a.dtype) for a in far]
        + [pltpu.SemaphoreType.DMA] * len(far),
        compiler_params=pltpu.CompilerParams(vmem_limit_bytes=min(held + 8 * MIB, 60 * MIB)),
        cost_estimate=pl.CostEstimate(flops=flops, bytes_accessed=moved, transcendentals=0),
        name=name,
    )(*scalars, *arrays, *far)


def shape(dims, dtype=BF16):
    return jax.ShapeDtypeStruct(dims, dtype)


def cut_copies(members, outs, group, piece, ids_ref, hidden_ref, sems):
    copies = []
    for (k, first), out in zip(members, outs):
        for block in range(out.shape[1] // piece):
            start = pl.multiple_of((block * group + ids_ref[k]) * piece, piece)
            source = hidden_ref.at[pl.ds(first, out.shape[0]), pl.ds(start, piece)]
            target = out.at[:, pl.ds(block * piece, piece)]
            copies.append(pltpu.make_async_copy(source, target, sems.at[len(copies)]))
            copies[len(copies) - 1].start()
    return copies


def cut_kernel(members, group, piece, ids_ref, hidden_ref, *refs):
    for copy in cut_copies(members, refs[: len(members)], group, piece, ids_ref, hidden_ref, refs[len(members)]):
        copy.wait()


def cut_plain(ids, hidden, k, group, piece):
    rows, depth = hidden.shape
    pieces = hidden.reshape(rows, depth // (group * piece), group, piece)
    return lax.dynamic_index_in_dim(pieces, ids[k], 2, keepdims=False).reshape(rows, depth // group)


def cut(ids, hidden, members, group, piece):
    depth = hidden.shape[1]
    if piece % 128:
        return [cut_plain(ids, hidden[first : first + count], k, group, piece) for k, first, count in members]
    number = len(members)
    return pl.pallas_call(
        functools.partial(cut_kernel, [(k, first) for k, first, _ in members], group, piece),
        out_shape=tuple(shape((count, depth // group)) for *_, count in members),
        in_specs=[SMEM, ANY],
        out_specs=(VMEM,) * number,
        scratch_shapes=[pltpu.SemaphoreType.DMA((number * depth // (group * piece),))],
        compiler_params=pltpu.CompilerParams(vmem_limit_bytes=8 * MIB),
        cost_estimate=pl.CostEstimate(flops=0, bytes_accessed=hidden.size * number, transcendentals=0),
        name="cut",
    )(ids, in_hbm(hidden))


def in_hbm(array):
    return pltpu.with_memory_space_constraint(array, pltpu.HBM)


def fetch(sources, slots):
    count = len(sources)
    copies = [pltpu.make_async_copy(sources[i], slots[i], slots[count + i]) for i in range(count)]
    for copy in copies:
        copy.start()
    return copies


def project_kernel(parts, carried, ids_ref, hidden_ref, *refs):
    weights, (slots, sems) = refs[: len(parts)], refs[len(refs) - 2 :]
    size = weights[0].shape[0]
    copies = []
    for number, part in enumerate(parts):
        start = pl.multiple_of(ids_ref[part] * size, size)
        source = hidden_ref.at[:, pl.ds(start, size)]
        copies.append(pltpu.make_async_copy(source, slots.at[number], sems.at[number]))
        copies[number].start()
    total = refs[len(parts)][...] if carried else None
    for number, weight in enumerate(weights):
        copies[number].wait()
        term = nn(slots[number], weight[...])
        total = term if total is None else total + term
    first = 0
    for out in refs[len(parts) + carried : len(refs) - 2]:
        width = out.shape[1]
        out[...] = total[:, first : first + width].astype(out.dtype)
        first += width


def project(ids, hidden, weights, total, widths, dtype):
    rows, size = hidden.shape[0], weights[0][0].shape[0]
    arrays = [array for array, *_ in weights] + total
    parts = [part for _, part, _ in weights]
    return pl.pallas_call(
        functools.partial(project_kernel, parts, len(total)),
        out_shape=tuple(shape((rows, width), dtype) for width in widths),
        in_specs=[SMEM, ANY] + [VMEM] * len(arrays),
        out_specs=(VMEM,) * len(widths),
        scratch_shapes=[pltpu.VMEM((len(parts), rows, size), BF16), pltpu.SemaphoreType.DMA((len(parts),))],
        compiler_params=pltpu.CompilerParams(vmem_limit_bytes=16 * MIB),
        cost_estimate=pl.CostEstimate(
            flops=2 * rows * size * len(parts) * sum(widths), bytes_accessed=4 * MIB, transcendentals=0
        ),
        name="project",
    )(ids, in_hbm(hidden), *arrays)


def hidden_kernel(places, ids_ref, grad_ref, *refs):
    count = len(places)
    slots = refs[count + 1 :]
    copies = fetch(refs[:count], slots)
    size = sum(slots[i].shape[0] for i in range(count) if places[i][0] == 0)
    for i, (part, first) in enumerate(places):
        rows = slots[i].shape[0]
        start = pl.multiple_of(ids_ref[part] * size + first, rows)
        copies[i].wait()
        refs[count][:, pl.ds(start, rows)] = nt(grad_ref[...], slots[i][...]).astype(BF16)


def hidden_grad(ids, grad, weights, depth):
    return pallas(
        functools.partial(hidden_kernel, [place for _, *place in weights]),
        shape((grad.shape[0], depth)),
        [ids],
        [grad],
        "hidden_grad",
        2 * grad.size * depth,
        far=[array for array, *_ in weights],
    )


def attend_kernel(layouts, group, rows, bq, bk, block_ref, pages_ref, *refs):
    count = sum(len(layout) for layout in layouts)
    parts, (grad_ref, own_ref) = refs[:count], refs[count : count + 2]
    q_ref, k_ref, v_ref, do_ref, s_ref, dp_ref, dk_ref, dv_ref, kt_ref, m_ref = refs[count + 2 :]
    seq, hd = do_ref.shape
    near = rows * group
    block = block_ref[0]
    scale = hd**-0.5
    scale2 = scale * math.log2(math.e)
    at = 0
    for layout, targets in zip(layouts, ((q_ref, k_ref), (v_ref,), (do_ref,))):
        for distances in layout:
            for number, distance in enumerate(distances):
                here = pl.ds(pl.multiple_of((block ^ distance) * rows, rows), rows)
                for column, target in enumerate(targets):
                    target[here, :] = parts[at][number * rows : (number + 1) * rows, column * hd : (column + 1) * hd]
            at += 1
    dk_ref[...] = jnp.zeros_like(dk_ref)
    dv_ref[...] = jnp.zeros_like(dv_ref)
    kt_ref[...] = k_ref[...].T
    ends, end = [], jnp.int32(0)
    for page in range(pages_ref.shape[1]):
        end = end + pages_ref[0, page]
        ends.append(end)
    low = lax.div(block, group) * near
    near_first, near_last = lax.div(low, bk), lax.div(low, bk) + near // bk

    def limit_of(pos):
        limit = jnp.full_like(pos, seq)
        for page_end in ends:
            limit = jnp.minimum(limit, jnp.where(page_end > pos, page_end, seq))
        return limit

    @pl.loop(0, seq // bq)
    def _(i):
        q0 = pl.multiple_of(i * bq, bq)
        limits = limit_of(q0 + lax.broadcasted_iota(jnp.int32, (1, bq), 1))
        count = lax.div(limit_of(q0 + (bq - 1)) + (bk - 1), bk)
        first, last = jnp.minimum(near_first, count), jnp.minimum(near_last, count)
        is_near = (q0 >= low) & (q0 < low + near)

        @pl.when(is_near | (first < last))
        def _():
            q = q_ref[pl.ds(q0, bq), :]
            do = do_ref[pl.ds(q0, bq), :]
            qt, dot_t = q.T, do.T

            def scores(masked, j, carry):
                row_max, total, dot = carry
                k0 = pl.multiple_of(j * bk, bk)
                s = nn(k_ref[pl.ds(k0, bk), :], qt) * scale2
                if masked:
                    key = k0 + lax.broadcasted_iota(jnp.int32, (bk, 1), 0)
                    s = jnp.where(key < limits, s, -1e30)
                high = jnp.maximum(row_max, jnp.max(s, axis=0, keepdims=True))
                p = jnp.exp2(s - high)
                dp = nn(v_ref[pl.ds(k0, bk), :], dot_t)
                s_ref[pl.ds(k0, bk), :] = p
                dp_ref[pl.ds(k0, bk), :] = dp
                m_ref[j] = high
                fade = jnp.exp2(row_max - high)
                total = total * fade + jnp.sum(p, axis=0, keepdims=True)
                dot = dot * fade + jnp.sum(p * dp, axis=0, keepdims=True)
                return high, total, dot

            zero = jnp.zeros((1, bq), F32)
            carry = (jnp.full((1, bq), -3e38, F32), zero, zero)
            full = jnp.minimum(lax.div(q0, bk), count)
            carry = lax.fori_loop(0, full, functools.partial(scores, False), carry)
            row_max, total, dot = lax.fori_loop(full, count, functools.partial(scores, True), carry)
            inv = 1.0 / total
            dot = dot * inv

            def dscore(j):
                k0 = pl.multiple_of(j * bk, bk)
                share = jnp.exp2(m_ref[j] - row_max) * inv
                gain = share * scale
                p = s_ref[pl.ds(k0, bk), :]
                return k0, p * share, (p * (dp_ref[pl.ds(k0, bk), :] * gain - dot * gain)).astype(BF16)

            def key_grads(j, carry):
                k0, p, ds = dscore(j)
                dv_ref[pl.ds(k0 - low, bk), :] += nn(p.astype(BF16), do)
                dk_ref[pl.ds(k0 - low, bk), :] += nn(ds, q)
                return carry

            def query_grads(j, dqt):
                k0, _, ds = dscore(j)
                return dqt + nn(kt_ref[:, pl.ds(k0, bk)], ds)

            def all_grads(j, dqt):
                k0, p, ds = dscore(j)
                dv_ref[pl.ds(k0 - low, bk), :] += nn(p.astype(BF16), do)
                dk_ref[pl.ds(k0 - low, bk), :] += nn(ds, q)
                return dqt + nn(kt_ref[:, pl.ds(k0, bk)], ds)

            @pl.when(is_near)
            def _():
                dqt = lax.fori_loop(0, first, query_grads, jnp.zeros((hd, bq), F32))
                dqt = lax.fori_loop(first, last, all_grads, dqt)
                dqt = lax.fori_loop(last, count, query_grads, dqt)
                grad_ref[pl.ds(pl.multiple_of(q0 - low, bq), bq), :hd] = dqt.T.astype(BF16)

            @pl.when(jnp.logical_not(is_near))
            def _():
                lax.fori_loop(first, last, key_grads, 0)

    grad_ref[:, hd : 2 * hd] = dk_ref[...].astype(BF16)
    grad_ref[:, 2 * hd :] = dv_ref[...].astype(BF16)
    own = pl.multiple_of(lax.rem(block, group) * rows, rows)
    own_ref[...] = grad_ref[pl.ds(own, rows), :]


def attend(block, pages, sets, blocks, group):
    rows = sets[0][0][0].shape[0] // len(sets[0][0][1])
    hd = sets[1][0][0].shape[1]
    seq, near = rows * blocks, rows * group
    bq, bk = (near, 2 * rows) if seq <= 4096 else (rows, rows)
    layouts = [[distances for _, distances in parts] for parts in sets]
    return pallas(
        functools.partial(attend_kernel, layouts, group, rows, bq, bk),
        (shape((near, 3 * hd)), shape((rows, 3 * hd))),
        [block, pages],
        [array for parts in sets for array, _ in parts],
        "attend",
        10 * seq * seq * hd,
        [pltpu.VMEM((seq, hd), BF16)] * 4
        + [pltpu.VMEM((seq, bq), F32)] * 2
        + [pltpu.VMEM((near, hd), F32)] * 2
        + [pltpu.VMEM((hd, seq), BF16), pltpu.VMEM((seq // bk, 1, bq), F32)],
    )


def weight_kernel(group, piece, places, ids_ref, fsdp_ref, grad_ref, hidden_ref, *refs):
    parts, (kept_ref, away_ref, own_ref, sems) = refs[: len(places)], refs[len(places) :]
    copies = cut_copies([(0, 0)], [own_ref], group, piece, ids_ref, hidden_ref, sems)
    rows, width = own_ref.shape
    fsdp_size = 2 * kept_ref.shape[0]
    size = width // fsdp_size
    for copy in copies:
        copy.wait()
    for j in range(fsdp_size):
        columns = pl.ds(pl.multiple_of(fsdp_ref[j] * size, size), size)
        total = None
        for (k, first), part in zip([(0, 0), *places], (own_ref, *parts)):
            count = part.shape[0]
            here = pl.ds(pl.multiple_of(ids_ref[k] * rows + first, math.gcd(rows, first)), count)
            term = tn(part[:, columns], grad_ref[here, :])
            total = term if total is None else total + term
        out = away_ref if j % 2 else kept_ref
        out[j // 2] = total.astype(out.dtype)


def weight_grad(ids, fsdp_ids, grad, hidden, parts, group, piece):
    fsdp_size, width = fsdp_ids.shape[0], grad.shape[1]
    rows, columns = hidden.shape[0], parts[0][0].shape[1]
    size = columns // fsdp_size
    half = (fsdp_size // 2, size, width)
    if piece % 128:
        parts = [(cut_plain(ids, hidden, 0, group, piece), 0, 0), *parts]
        total = sum(
            tn(array, lax.dynamic_slice_in_dim(grad, ids[k] * rows + first, array.shape[0], 0))
            for array, k, first in parts
        )
        both = jnp.take(total.reshape(fsdp_size, size, width), fsdp_ids, axis=0)
        both = both.reshape(fsdp_size // 2, 2, size, width)
        return both[:, 0], both[:, 1].astype(BF16)
    return pl.pallas_call(
        functools.partial(weight_kernel, group, piece, [(k, first) for _, k, first in parts]),
        out_shape=(shape(half, F32), shape(half)),
        in_specs=[SMEM, SMEM, VMEM, ANY] + [VMEM] * len(parts),
        out_specs=(VMEM, VMEM),
        scratch_shapes=[pltpu.VMEM((rows, columns), BF16), pltpu.SemaphoreType.DMA((columns // piece,))],
        compiler_params=pltpu.CompilerParams(vmem_limit_bytes=20 * MIB),
        cost_estimate=pl.CostEstimate(flops=2 * grad.size * columns, bytes_accessed=8 * MIB, transcendentals=0),
        name="weight_grad",
    )(ids, fsdp_ids, grad, hidden, *[array for array, *_ in parts])


def finish_kernel(group, piece, ids_ref, *refs):
    out_ref = refs[len(refs) - 1]
    for number, block in enumerate(refs[: len(refs) - 1]):
        count = block.shape[0] // piece
        for i in range(count):
            place = (number // group * count + i) * group + ids_ref[number % group]
            start = pl.multiple_of(place * piece, piece)
            out_ref[pl.ds(start, piece), :] = block[i * piece : (i + 1) * piece, :].astype(F32)


def finish(ids, blocks, group, piece):
    rows, width = blocks[0].shape
    if piece % 16:
        order = jnp.stack(blocks).reshape(-1, group, rows // piece, piece, width)
        order = jnp.take(order, ids, axis=1).swapaxes(1, 2)
        return order.reshape(len(blocks) * rows, width).astype(F32)
    return pallas(
        functools.partial(finish_kernel, group, piece),
        shape((len(blocks) * rows, width), F32),
        [ids],
        blocks,
        "finish",
        0,
    )


def swap(array, axis, size, distance):
    return lax.ppermute(array, axis, [(i, i ^ distance) for i in range(size)])


def spread(part, size):
    array, distances = part
    return [(swap(array, "ctx", size, k), [k ^ d for d in distances]) for k in range(2, size, 2)]


def widen(parts, size):
    arrays = [array for array, _ in parts]
    whole = jnp.concatenate(arrays, axis=0) if len(arrays) > 1 else arrays[0]
    return swap(whole, "ctx", size, 1), [1 ^ d for _, distances in parts for d in distances]


def after(part, done):
    array, *_ = lax.optimization_barrier((part[0], *[other for other, _ in done]))
    return array, part[1]


def local(ctx_size, fsdp_size, hidden_in, page_tokens, grad_attn, w_qkv):
    hidden, grad_out = hidden_in[0], grad_attn[0]
    rows, depth = hidden.shape
    hd = grad_out.shape[1]
    f, c = lax.axis_index("fsdp"), lax.axis_index("ctx")
    fsdp_ids = f ^ jnp.arange(fsdp_size, dtype=jnp.int32)
    group = min(4, ctx_size)
    group_ids = (c % group) ^ jnp.arange(group, dtype=jnp.int32)

    piece = depth // (fsdp_size * ctx_size)
    top = fsdp_size // 2
    weights = {0: [w_qkv], top: [swap(w_qkv, "fsdp", fsdp_size, top)]}
    near = rows * 3 // 4
    members = [(1, 0, rows), (2, 0, near), (2, near, rows - near)]
    chunks = cut(group_ids, hidden, members, group, piece)
    grads = [(grad_out, [0])]
    grads += spread(grads[0], ctx_size)
    moved = [swap(chunk, "ctx", ctx_size, k) for chunk, (k, *_) in zip(chunks[:2], members)]
    arrays, _ = lax.optimization_barrier(([array for array, _ in grads], chunks))
    grads = [(array, distances) for array, (_, distances) in zip(arrays, grads)]
    whole = jnp.concatenate([array for array, _ in grads], axis=0)
    array, distances = widen([(whole, [d for _, distances in grads for d in distances])], ctx_size)
    weights[1] = [swap(w_qkv, "fsdp", fsdp_size, 1)]
    early = [(weights[k][0], k, 0) for k in (0, 1)]
    (total,) = project(fsdp_ids, hidden, early, [], (3 * hd,), F32)
    weights[top], array, total = lax.optimization_barrier((weights[top], array, total))
    grads.append((array, distances))
    bit = top // 2
    while bit:
        for k in list(weights):
            if k ^ bit not in weights:
                weights[k ^ bit] = [swap(weights[k][0], "fsdp", fsdp_size, bit)]
        bit //= 2
    weights = [(weights[k][0], k, 0) for k in range(fsdp_size)]

    qk, v = project(fsdp_ids, hidden, weights[2:], [total], (2 * hd, hd), BF16)
    qks = [(qk, [0])]
    qks += spread(qks[0], ctx_size)
    v_pair = [(v, [0]), widen([after((v, [0]), [(moved[0], 0)])], ctx_size)]
    pair = jnp.concatenate([array for array, _ in v_pair], axis=0), [0, 1]
    vs = [pair, *spread(after(pair, qks[1:]), ctx_size)]
    qks.append(widen([after(qks[0], [pair, (moved[0], 0), (moved[1], 0)]), *qks[1:]], ctx_size))
    moved.append(swap(after((chunks[2], 0), qks[1 : ctx_size // 2])[0], "ctx", ctx_size, 2))
    members.append((3, 0, rows))
    (late,) = cut(group_ids, after((hidden, 0), [(qk, 0)])[0], members[3:], group, piece)
    moved.append(swap(after((late, 0), [qks[-1], vs[1]])[0], "ctx", ctx_size, 3))
    block = c.reshape(1).astype(jnp.int32)
    grad_near, grad_own = attend(block, page_tokens, [qks, vs, grads], ctx_size, group)
    parts = [(array, k, first) for array, (k, first, _) in zip(moved, members)]
    kept, away = weight_grad(group_ids, fsdp_ids, grad_near, hidden, parts, group, piece)
    bit = 1
    while bit < top:
        total = kept + swap(away, "fsdp", fsdp_size, bit).astype(F32)
        bit *= 2
        kept, away = total[0::2], total[1::2].astype(BF16)
    half = kept.shape[1] // 2
    first = swap(away[0, :half], "fsdp", fsdp_size, top)
    second, first = lax.optimization_barrier((away[0, half:], first))
    second = swap(second, "fsdp", fsdp_size, top)
    totals = [kept[0, :half] + first.astype(F32)]
    rest, total = lax.optimization_barrier((kept[0, half:], totals[0].astype(BF16)))
    grad_own, total = lax.optimization_barrier((grad_own, total))
    grad_inputs = hidden_grad(fsdp_ids, grad_own, weights, depth)
    second, grad_inputs = lax.optimization_barrier((second, grad_inputs))
    totals = [total, rest + second.astype(F32)]
    bit = group
    while bit < ctx_size:
        sent = [total.astype(BF16) for total in totals]
        totals = [own.astype(F32) + swap(own, "ctx", ctx_size, bit).astype(F32) for own in sent]
        bit *= 2
    totals = [total.astype(BF16) for total in totals]
    gathered = [swap(total, "ctx", ctx_size, k) if k else total for total in totals for k in range(group)]
    grad_weights = finish(group_ids, gathered, group, piece)
    return grad_inputs[None], grad_weights


def solution(mesh):
    in_specs = (P("fsdp", "ctx", None), P("fsdp", None), P("fsdp", "ctx", None), P("fsdp", None))
    out_specs = (P("fsdp", "ctx", None), P("fsdp", None))
    body = functools.partial(local, mesh.shape["ctx"], mesh.shape["fsdp"])
    return jax.shard_map(body, mesh=mesh, in_specs=in_specs, out_specs=out_specs, check_vma=False)
```

```python
import functools
import math

import jax
import jax.numpy as jnp
from jax import lax
from jax.experimental import pallas as pl
from jax.experimental.pallas import tpu as pltpu
from jax.sharding import PartitionSpec as P

F32 = jnp.float32
BF16 = jnp.bfloat16
VMEM = pl.BlockSpec(memory_space=pltpu.VMEM)
SMEM = pl.BlockSpec(memory_space=pltpu.SMEM)
ANY = pl.BlockSpec(memory_space=pltpu.HBM)
MIB = 1024 * 1024


def nt(left, right):
    return lax.dot_general(left, right, (((1,), (1,)), ((), ())), preferred_element_type=F32)


def nn(left, right):
    return jnp.dot(left, right, preferred_element_type=F32)


def tn(left, right):
    return lax.dot_general(left, right, (((0,), (0,)), ((), ())), preferred_element_type=F32)


def pallas(kernel, out_shape, scalars, arrays, name, flops, scratch=(), far=()):
    outs = out_shape if isinstance(out_shape, tuple) else (out_shape,)
    moved = sum(a.size * a.dtype.itemsize for a in (*arrays, *far, *outs))
    held = moved + sum(math.prod(a.shape) * jnp.dtype(a.dtype).itemsize for a in scratch)
    return pl.pallas_call(
        kernel,
        out_shape=out_shape,
        in_specs=[SMEM] * len(scalars) + [VMEM] * len(arrays) + [ANY] * len(far),
        out_specs=jax.tree.map(lambda _: VMEM, out_shape),
        scratch_shapes=[*scratch]
        + [pltpu.VMEM(a.shape, a.dtype) for a in far]
        + [pltpu.SemaphoreType.DMA] * len(far),
        compiler_params=pltpu.CompilerParams(vmem_limit_bytes=min(held + 8 * MIB, 60 * MIB)),
        cost_estimate=pl.CostEstimate(flops=flops, bytes_accessed=moved, transcendentals=0),
        name=name,
    )(*scalars, *arrays, *far)


def shape(dims, dtype=BF16):
    return jax.ShapeDtypeStruct(dims, dtype)


def cut_copies(members, outs, group, piece, ids_ref, hidden_ref, sems):
    copies = []
    for (k, first), out in zip(members, outs):
        for block in range(out.shape[1] // piece):
            start = pl.multiple_of((block * group + ids_ref[k]) * piece, piece)
            source = hidden_ref.at[pl.ds(first, out.shape[0]), pl.ds(start, piece)]
            target = out.at[:, pl.ds(block * piece, piece)]
            copies.append(pltpu.make_async_copy(source, target, sems.at[len(copies)]))
            copies[len(copies) - 1].start()
    return copies


def cut_kernel(members, group, piece, ids_ref, hidden_ref, *refs):
    for copy in cut_copies(members, refs[: len(members)], group, piece, ids_ref, hidden_ref, refs[len(members)]):
        copy.wait()


def cut_plain(ids, hidden, k, group, piece):
    rows, depth = hidden.shape
    pieces = hidden.reshape(rows, depth // (group * piece), group, piece)
    return lax.dynamic_index_in_dim(pieces, ids[k], 2, keepdims=False).reshape(rows, depth // group)


def cut(ids, hidden, members, group, piece):
    depth = hidden.shape[1]
    if piece % 128:
        return [cut_plain(ids, hidden[first : first + count], k, group, piece) for k, first, count in members]
    number = len(members)
    return pl.pallas_call(
        functools.partial(cut_kernel, [(k, first) for k, first, _ in members], group, piece),
        out_shape=tuple(shape((count, depth // group)) for *_, count in members),
        in_specs=[SMEM, ANY],
        out_specs=(VMEM,) * number,
        scratch_shapes=[pltpu.SemaphoreType.DMA((number * depth // (group * piece),))],
        compiler_params=pltpu.CompilerParams(vmem_limit_bytes=8 * MIB),
        cost_estimate=pl.CostEstimate(flops=0, bytes_accessed=hidden.size * number, transcendentals=0),
        name="cut",
    )(ids, in_hbm(hidden))


def in_hbm(array):
    return pltpu.with_memory_space_constraint(array, pltpu.HBM)


def fetch(sources, slots):
    count = len(sources)
    copies = [pltpu.make_async_copy(sources[i], slots[i], slots[count + i]) for i in range(count)]
    for copy in copies:
        copy.start()
    return copies


def project_kernel(parts, carried, ids_ref, hidden_ref, *refs):
    weights, (slots, sems) = refs[: len(parts)], refs[len(refs) - 2 :]
    size = weights[0].shape[0]
    copies = []
    for number, part in enumerate(parts):
        start = pl.multiple_of(ids_ref[part] * size, size)
        source = hidden_ref.at[:, pl.ds(start, size)]
        copies.append(pltpu.make_async_copy(source, slots.at[number], sems.at[number]))
        copies[number].start()
    total = refs[len(parts)][...] if carried else None
    for number, weight in enumerate(weights):
        copies[number].wait()
        term = nn(slots[number], weight[...])
        total = term if total is None else total + term
    first = 0
    for out in refs[len(parts) + carried : len(refs) - 2]:
        width = out.shape[1]
        out[...] = total[:, first : first + width].astype(out.dtype)
        first += width


def project(ids, hidden, weights, total, widths, dtype):
    rows, size = hidden.shape[0], weights[0][0].shape[0]
    arrays = [array for array, *_ in weights] + total
    parts = [part for _, part, _ in weights]
    return pl.pallas_call(
        functools.partial(project_kernel, parts, len(total)),
        out_shape=tuple(shape((rows, width), dtype) for width in widths),
        in_specs=[SMEM, ANY] + [VMEM] * len(arrays),
        out_specs=(VMEM,) * len(widths),
        scratch_shapes=[pltpu.VMEM((len(parts), rows, size), BF16), pltpu.SemaphoreType.DMA((len(parts),))],
        compiler_params=pltpu.CompilerParams(vmem_limit_bytes=16 * MIB),
        cost_estimate=pl.CostEstimate(
            flops=2 * rows * size * len(parts) * sum(widths), bytes_accessed=4 * MIB, transcendentals=0
        ),
        name="project",
    )(ids, in_hbm(hidden), *arrays)


def hidden_kernel(places, ids_ref, grad_ref, *refs):
    count = len(places)
    slots = refs[count + 1 :]
    copies = fetch(refs[:count], slots)
    size = sum(slots[i].shape[0] for i in range(count) if places[i][0] == 0)
    for i, (part, first) in enumerate(places):
        rows = slots[i].shape[0]
        start = pl.multiple_of(ids_ref[part] * size + first, rows)
        copies[i].wait()
        refs[count][:, pl.ds(start, rows)] = nt(grad_ref[...], slots[i][...]).astype(BF16)


def hidden_grad(ids, grad, weights, depth):
    return pallas(
        functools.partial(hidden_kernel, [place for _, *place in weights]),
        shape((grad.shape[0], depth)),
        [ids],
        [grad],
        "hidden_grad",
        2 * grad.size * depth,
        far=[array for array, *_ in weights],
    )


def attend_kernel(layouts, group, rows, bq, bk, block_ref, pages_ref, *refs):
    count = sum(len(layout) for layout in layouts)
    parts, (grad_ref, own_ref) = refs[:count], refs[count : count + 2]
    q_ref, k_ref, v_ref, do_ref, s_ref, dp_ref, dk_ref, dv_ref, kt_ref, m_ref = refs[count + 2 :]
    seq, hd = do_ref.shape
    near = rows * group
    block = block_ref[0]
    scale = hd**-0.5
    scale2 = scale * math.log2(math.e)
    at = 0
    for layout, targets in zip(layouts, ((q_ref, k_ref), (v_ref,), (do_ref,))):
        for distances in layout:
            for number, distance in enumerate(distances):
                here = pl.ds(pl.multiple_of((block ^ distance) * rows, rows), rows)
                for column, target in enumerate(targets):
                    target[here, :] = parts[at][number * rows : (number + 1) * rows, column * hd : (column + 1) * hd]
            at += 1
    dk_ref[...] = jnp.zeros_like(dk_ref)
    dv_ref[...] = jnp.zeros_like(dv_ref)
    kt_ref[...] = k_ref[...].T
    ends, end = [], jnp.int32(0)
    for page in range(pages_ref.shape[1]):
        end = end + pages_ref[0, page]
        ends.append(end)
    low = lax.div(block, group) * near
    near_first, near_last = lax.div(low, bk), lax.div(low, bk) + near // bk

    def limit_of(pos):
        limit = jnp.full_like(pos, seq)
        for page_end in ends:
            limit = jnp.minimum(limit, jnp.where(page_end > pos, page_end, seq))
        return limit

    @pl.loop(0, seq // bq)
    def _(i):
        q0 = pl.multiple_of(i * bq, bq)
        limits = limit_of(q0 + lax.broadcasted_iota(jnp.int32, (1, bq), 1))
        count = lax.div(limit_of(q0 + (bq - 1)) + (bk - 1), bk)
        first, last = jnp.minimum(near_first, count), jnp.minimum(near_last, count)
        is_near = (q0 >= low) & (q0 < low + near)

        @pl.when(is_near | (first < last))
        def _():
            q = q_ref[pl.ds(q0, bq), :]
            do = do_ref[pl.ds(q0, bq), :]
            qt, dot_t = q.T, do.T

            def scores(masked, j, carry):
                row_max, total, dot = carry
                k0 = pl.multiple_of(j * bk, bk)
                s = nn(k_ref[pl.ds(k0, bk), :], qt) * scale2
                if masked:
                    key = k0 + lax.broadcasted_iota(jnp.int32, (bk, 1), 0)
                    s = jnp.where(key < limits, s, -1e30)
                high = jnp.maximum(row_max, jnp.max(s, axis=0, keepdims=True))
                p = jnp.exp2(s - high)
                dp = nn(v_ref[pl.ds(k0, bk), :], dot_t)
                s_ref[pl.ds(k0, bk), :] = p
                dp_ref[pl.ds(k0, bk), :] = dp
                m_ref[j] = high
                fade = jnp.exp2(row_max - high)
                total = total * fade + jnp.sum(p, axis=0, keepdims=True)
                dot = dot * fade + jnp.sum(p * dp, axis=0, keepdims=True)
                return high, total, dot

            zero = jnp.zeros((1, bq), F32)
            carry = (jnp.full((1, bq), -3e38, F32), zero, zero)
            full = jnp.minimum(lax.div(q0, bk), count)
            carry = lax.fori_loop(0, full, functools.partial(scores, False), carry)
            row_max, total, dot = lax.fori_loop(full, count, functools.partial(scores, True), carry)
            inv = 1.0 / total
            dot = dot * inv

            def dscore(j):
                k0 = pl.multiple_of(j * bk, bk)
                share = jnp.exp2(m_ref[j] - row_max) * inv
                gain = share * scale
                p = s_ref[pl.ds(k0, bk), :]
                return k0, p * share, (p * (dp_ref[pl.ds(k0, bk), :] * gain - dot * gain)).astype(BF16)

            def key_grads(j, carry):
                k0, p, ds = dscore(j)
                dv_ref[pl.ds(k0 - low, bk), :] += nn(p.astype(BF16), do)
                dk_ref[pl.ds(k0 - low, bk), :] += nn(ds, q)
                return carry

            def query_grads(j, dqt):
                k0, _, ds = dscore(j)
                return dqt + nn(kt_ref[:, pl.ds(k0, bk)], ds)

            def all_grads(j, dqt):
                k0, p, ds = dscore(j)
                dv_ref[pl.ds(k0 - low, bk), :] += nn(p.astype(BF16), do)
                dk_ref[pl.ds(k0 - low, bk), :] += nn(ds, q)
                return dqt + nn(kt_ref[:, pl.ds(k0, bk)], ds)

            @pl.when(is_near)
            def _():
                dqt = lax.fori_loop(0, first, query_grads, jnp.zeros((hd, bq), F32))
                dqt = lax.fori_loop(first, last, all_grads, dqt)
                dqt = lax.fori_loop(last, count, query_grads, dqt)
                grad_ref[pl.ds(pl.multiple_of(q0 - low, bq), bq), :hd] = dqt.T.astype(BF16)

            @pl.when(jnp.logical_not(is_near))
            def _():
                lax.fori_loop(first, last, key_grads, 0)

    grad_ref[:, hd : 2 * hd] = dk_ref[...].astype(BF16)
    grad_ref[:, 2 * hd :] = dv_ref[...].astype(BF16)
    own = pl.multiple_of(lax.rem(block, group) * rows, rows)
    own_ref[...] = grad_ref[pl.ds(own, rows), :]


def attend(block, pages, sets, blocks, group):
    rows = sets[0][0][0].shape[0] // len(sets[0][0][1])
    hd = sets[1][0][0].shape[1]
    seq, near = rows * blocks, rows * group
    bq, bk = (near, 2 * rows) if seq <= 4096 else (rows, rows)
    layouts = [[distances for _, distances in parts] for parts in sets]
    return pallas(
        functools.partial(attend_kernel, layouts, group, rows, bq, bk),
        (shape((near, 3 * hd)), shape((rows, 3 * hd))),
        [block, pages],
        [array for parts in sets for array, _ in parts],
        "attend",
        10 * seq * seq * hd,
        [pltpu.VMEM((seq, hd), BF16)] * 4
        + [pltpu.VMEM((seq, bq), F32)] * 2
        + [pltpu.VMEM((near, hd), F32)] * 2
        + [pltpu.VMEM((hd, seq), BF16), pltpu.VMEM((seq // bk, 1, bq), F32)],
    )


def weight_kernel(group, piece, places, ids_ref, fsdp_ref, grad_ref, hidden_ref, *refs):
    parts, (kept_ref, away_ref, own_ref, sems) = refs[: len(places)], refs[len(places) :]
    copies = cut_copies([(0, 0)], [own_ref], group, piece, ids_ref, hidden_ref, sems)
    rows, width = own_ref.shape
    fsdp_size = 2 * kept_ref.shape[0]
    size = width // fsdp_size
    for copy in copies:
        copy.wait()
    for j in range(fsdp_size):
        columns = pl.ds(pl.multiple_of(fsdp_ref[j] * size, size), size)
        total = None
        for (k, first), part in zip([(0, 0), *places], (own_ref, *parts)):
            count = part.shape[0]
            here = pl.ds(pl.multiple_of(ids_ref[k] * rows + first, math.gcd(rows, first)), count)
            term = tn(part[:, columns], grad_ref[here, :])
            total = term if total is None else total + term
        out = away_ref if j % 2 else kept_ref
        out[j // 2] = total.astype(out.dtype)


def weight_grad(ids, fsdp_ids, grad, hidden, parts, group, piece):
    fsdp_size, width = fsdp_ids.shape[0], grad.shape[1]
    rows, columns = hidden.shape[0], parts[0][0].shape[1]
    size = columns // fsdp_size
    half = (fsdp_size // 2, size, width)
    if piece % 128:
        parts = [(cut_plain(ids, hidden, 0, group, piece), 0, 0), *parts]
        total = sum(
            tn(array, lax.dynamic_slice_in_dim(grad, ids[k] * rows + first, array.shape[0], 0))
            for array, k, first in parts
        )
        both = jnp.take(total.reshape(fsdp_size, size, width), fsdp_ids, axis=0)
        both = both.reshape(fsdp_size // 2, 2, size, width)
        return both[:, 0], both[:, 1].astype(BF16)
    return pl.pallas_call(
        functools.partial(weight_kernel, group, piece, [(k, first) for _, k, first in parts]),
        out_shape=(shape(half, F32), shape(half)),
        in_specs=[SMEM, SMEM, VMEM, ANY] + [VMEM] * len(parts),
        out_specs=(VMEM, VMEM),
        scratch_shapes=[pltpu.VMEM((rows, columns), BF16), pltpu.SemaphoreType.DMA((columns // piece,))],
        compiler_params=pltpu.CompilerParams(vmem_limit_bytes=20 * MIB),
        cost_estimate=pl.CostEstimate(flops=2 * grad.size * columns, bytes_accessed=8 * MIB, transcendentals=0),
        name="weight_grad",
    )(ids, fsdp_ids, grad, hidden, *[array for array, *_ in parts])


def finish_kernel(group, piece, turn, ids_ref, *refs):
    blocks, (out_ref, wide_ref, sems) = refs[:group], refs[len(refs) - 3 :]
    copies = []
    for number, block in enumerate(blocks):
        count = block.shape[0] // piece
        for i in range(count):
            place = (turn * count + i) * group + ids_ref[number]
            here = pl.ds(pl.multiple_of(place * piece, piece), piece)
            slot = wide_ref.at[len(copies)]
            slot[...] = block[i * piece : (i + 1) * piece, :].astype(F32)
            copies.append(pltpu.make_async_copy(slot, out_ref.at[here, :], sems.at[len(copies)]))
            copies[len(copies) - 1].start()
    for copy in copies:
        copy.wait()


def finish(ids, blocks, group, piece):
    rows, width = blocks[0].shape
    if piece % 16:
        order = jnp.stack(blocks).reshape(-1, group, rows // piece, piece, width)
        order = jnp.take(order, ids, axis=1).swapaxes(1, 2)
        return order.reshape(len(blocks) * rows, width).astype(F32)
    out = []
    for turn in range(len(blocks) // group):
        number = group * rows // piece
        out = pl.pallas_call(
            functools.partial(finish_kernel, group, piece, turn),
            out_shape=shape((len(blocks) * rows, width), F32),
            in_specs=[SMEM] + [VMEM] * group + [ANY] * (turn > 0),
            out_specs=ANY,
            input_output_aliases={group + 1: 0} if turn else {},
            scratch_shapes=[pltpu.VMEM((number, piece, width), F32), pltpu.SemaphoreType.DMA((number,))],
            compiler_params=pltpu.CompilerParams(vmem_limit_bytes=12 * MIB),
            cost_estimate=pl.CostEstimate(flops=0, bytes_accessed=3 * MIB, transcendentals=0),
            name="finish",
        )(ids, *blocks[turn * group : (turn + 1) * group], *([out] if turn else []))
    return out


def swap(array, axis, size, distance):
    return lax.ppermute(array, axis, [(i, i ^ distance) for i in range(size)])


def spread(part, size):
    array, distances = part
    return [(swap(array, "ctx", size, k), [k ^ d for d in distances]) for k in range(2, size, 2)]


def widen(parts, size):
    arrays = [array for array, _ in parts]
    whole = jnp.concatenate(arrays, axis=0) if len(arrays) > 1 else arrays[0]
    return swap(whole, "ctx", size, 1), [1 ^ d for _, distances in parts for d in distances]


def after(part, done):
    array, *_ = lax.optimization_barrier((part[0], *[other for other, _ in done]))
    return array, part[1]


def local(ctx_size, fsdp_size, hidden_in, page_tokens, grad_attn, w_qkv):
    hidden, grad_out = hidden_in[0], grad_attn[0]
    rows, depth = hidden.shape
    hd = grad_out.shape[1]
    f, c = lax.axis_index("fsdp"), lax.axis_index("ctx")
    fsdp_ids = f ^ jnp.arange(fsdp_size, dtype=jnp.int32)
    group = min(4, ctx_size)
    group_ids = (c % group) ^ jnp.arange(group, dtype=jnp.int32)

    piece = depth // (fsdp_size * ctx_size)
    top = fsdp_size // 2
    weights = {0: [w_qkv], top: [swap(w_qkv, "fsdp", fsdp_size, top)]}
    near = rows * 5 // 8
    members = [(1, 0, rows), (2, 0, near), (2, near, rows - near)]
    chunks = cut(group_ids, hidden, members, group, piece)
    grads = [(grad_out, [0])]
    grads += spread(grads[0], ctx_size)
    moved = [swap(chunk, "ctx", ctx_size, k) for chunk, (k, *_) in zip(chunks[:2], members)]
    arrays, _ = lax.optimization_barrier(([array for array, _ in grads], chunks))
    grads = [(array, distances) for array, (_, distances) in zip(arrays, grads)]
    whole = jnp.concatenate([array for array, _ in grads], axis=0)
    array, distances = widen([(whole, [d for _, distances in grads for d in distances])], ctx_size)
    weights[1] = [swap(w_qkv, "fsdp", fsdp_size, 1)]
    early = [(weights[k][0], k, 0) for k in (0, 1)]
    (total,) = project(fsdp_ids, hidden, early, [], (3 * hd,), F32)
    weights[top], array, total = lax.optimization_barrier((weights[top], array, total))
    grads.append((array, distances))
    bit = top // 2
    while bit:
        for k in list(weights):
            if k ^ bit not in weights:
                weights[k ^ bit] = [swap(weights[k][0], "fsdp", fsdp_size, bit)]
        bit //= 2
    weights = [(weights[k][0], k, 0) for k in range(fsdp_size)]

    qk, v = project(fsdp_ids, hidden, weights[2:], [total], (2 * hd, hd), BF16)
    qks = [(qk, [0])]
    qks += spread(qks[0], ctx_size)
    v_pair = [(v, [0]), widen([after((v, [0]), [(moved[0], 0)])], ctx_size)]
    pair = jnp.concatenate([array for array, _ in v_pair], axis=0), [0, 1]
    vs = [pair, *spread(after(pair, qks[1:]), ctx_size)]
    qks.append(widen([after(qks[0], [pair, (moved[0], 0), (moved[1], 0)]), *qks[1:]], ctx_size))
    moved.append(swap(after((chunks[2], 0), qks[1 : ctx_size // 2])[0], "ctx", ctx_size, 2))
    members.append((3, 0, rows))
    (late,) = cut(group_ids, after((hidden, 0), [(qk, 0)])[0], members[3:], group, piece)
    moved.append(swap(after((late, 0), [qks[-1], vs[1]])[0], "ctx", ctx_size, 3))
    block = c.reshape(1).astype(jnp.int32)
    grad_near, grad_own = attend(block, page_tokens, [qks, vs, grads], ctx_size, group)
    parts = [(array, k, first) for array, (k, first, _) in zip(moved, members)]
    kept, away = weight_grad(group_ids, fsdp_ids, grad_near, hidden, parts, group, piece)
    bit = 1
    while bit < top:
        total = kept + swap(away, "fsdp", fsdp_size, bit).astype(F32)
        bit *= 2
        kept, away = total[0::2], total[1::2].astype(BF16)
    half = kept.shape[1] // 2
    first = swap(away[0, :half], "fsdp", fsdp_size, top)
    second, first = lax.optimization_barrier((away[0, half:], first))
    second = swap(second, "fsdp", fsdp_size, top)
    totals = [kept[0, :half] + first.astype(F32)]
    rest, total = lax.optimization_barrier((kept[0, half:], totals[0].astype(BF16)))
    grad_own, total = lax.optimization_barrier((grad_own, total))
    grad_inputs = hidden_grad(fsdp_ids, grad_own, weights, depth)
    second, grad_inputs = lax.optimization_barrier((second, grad_inputs))
    totals = [total, rest + second.astype(F32)]
    bit = group
    while bit < ctx_size:
        sent = [total.astype(BF16) for total in totals]
        totals = [own.astype(F32) + swap(own, "ctx", ctx_size, bit).astype(F32) for own in sent]
        bit *= 2
    totals = [total.astype(BF16) for total in totals]
    gathered = [swap(total, "ctx", ctx_size, k) if k else total for total in totals for k in range(group)]
    grad_weights = finish(group_ids, gathered, group, piece)
    return grad_inputs[None], grad_weights


def solution(mesh):
    in_specs = (P("fsdp", "ctx", None), P("fsdp", None), P("fsdp", "ctx", None), P("fsdp", None))
    out_specs = (P("fsdp", "ctx", None), P("fsdp", None))
    body = functools.partial(local, mesh.shape["ctx"], mesh.shape["fsdp"])
    return jax.shard_map(body, mesh=mesh, in_specs=in_specs, out_specs=out_specs, check_vma=False)
```

```python
import functools
import math

import jax
import jax.numpy as jnp
from jax import lax
from jax.experimental import pallas as pl
from jax.experimental.pallas import tpu as pltpu
from jax.sharding import PartitionSpec as P

F32 = jnp.float32
BF16 = jnp.bfloat16
VMEM = pl.BlockSpec(memory_space=pltpu.VMEM)
SMEM = pl.BlockSpec(memory_space=pltpu.SMEM)
ANY = pl.BlockSpec(memory_space=pltpu.HBM)
MIB = 1024 * 1024


def nt(left, right):
    return lax.dot_general(left, right, (((1,), (1,)), ((), ())), preferred_element_type=F32)


def nn(left, right):
    return jnp.dot(left, right, preferred_element_type=F32)


def tn(left, right):
    return lax.dot_general(left, right, (((0,), (0,)), ((), ())), preferred_element_type=F32)


def pallas(kernel, out_shape, scalars, arrays, name, flops, scratch=(), far=()):
    outs = out_shape if isinstance(out_shape, tuple) else (out_shape,)
    moved = sum(a.size * a.dtype.itemsize for a in (*arrays, *far, *outs))
    held = moved + sum(math.prod(a.shape) * jnp.dtype(a.dtype).itemsize for a in scratch)
    return pl.pallas_call(
        kernel,
        out_shape=out_shape,
        in_specs=[SMEM] * len(scalars) + [VMEM] * len(arrays) + [ANY] * len(far),
        out_specs=jax.tree.map(lambda _: VMEM, out_shape),
        scratch_shapes=[*scratch]
        + [pltpu.VMEM(a.shape, a.dtype) for a in far]
        + [pltpu.SemaphoreType.DMA] * len(far),
        compiler_params=pltpu.CompilerParams(vmem_limit_bytes=min(held + 8 * MIB, 60 * MIB)),
        cost_estimate=pl.CostEstimate(flops=flops, bytes_accessed=moved, transcendentals=0),
        name=name,
    )(*scalars, *arrays, *far)


def shape(dims, dtype=BF16):
    return jax.ShapeDtypeStruct(dims, dtype)


def cut_copies(members, outs, group, piece, ids_ref, hidden_ref, sems):
    copies = []
    for (k, first), out in zip(members, outs):
        for block in range(out.shape[1] // piece):
            start = pl.multiple_of((block * group + ids_ref[k]) * piece, piece)
            source = hidden_ref.at[pl.ds(first, out.shape[0]), pl.ds(start, piece)]
            target = out.at[:, pl.ds(block * piece, piece)]
            copies.append(pltpu.make_async_copy(source, target, sems.at[len(copies)]))
            copies[len(copies) - 1].start()
    return copies


def cut_kernel(members, group, piece, ids_ref, hidden_ref, *refs):
    for copy in cut_copies(members, refs[: len(members)], group, piece, ids_ref, hidden_ref, refs[len(members)]):
        copy.wait()


def cut_plain(ids, hidden, k, group, piece):
    rows, depth = hidden.shape
    pieces = hidden.reshape(rows, depth // (group * piece), group, piece)
    return lax.dynamic_index_in_dim(pieces, ids[k], 2, keepdims=False).reshape(rows, depth // group)


def cut(ids, hidden, members, group, piece):
    depth = hidden.shape[1]
    if piece % 128:
        return [cut_plain(ids, hidden[first : first + count], k, group, piece) for k, first, count in members]
    number = len(members)
    return pl.pallas_call(
        functools.partial(cut_kernel, [(k, first) for k, first, _ in members], group, piece),
        out_shape=tuple(shape((count, depth // group)) for *_, count in members),
        in_specs=[SMEM, ANY],
        out_specs=(VMEM,) * number,
        scratch_shapes=[pltpu.SemaphoreType.DMA((number * depth // (group * piece),))],
        compiler_params=pltpu.CompilerParams(vmem_limit_bytes=8 * MIB),
        cost_estimate=pl.CostEstimate(flops=0, bytes_accessed=hidden.size * number, transcendentals=0),
        name="cut",
    )(ids, in_hbm(hidden))


def in_hbm(array):
    return pltpu.with_memory_space_constraint(array, pltpu.HBM)


def fetch(sources, slots):
    count = len(sources)
    copies = [pltpu.make_async_copy(sources[i], slots[i], slots[count + i]) for i in range(count)]
    for copy in copies:
        copy.start()
    return copies


def project_kernel(parts, carried, ids_ref, hidden_ref, *refs):
    weights, (slots, sems) = refs[: len(parts)], refs[len(refs) - 2 :]
    size = weights[0].shape[0]
    copies = []
    for number, part in enumerate(parts):
        start = pl.multiple_of(ids_ref[part] * size, size)
        source = hidden_ref.at[:, pl.ds(start, size)]
        copies.append(pltpu.make_async_copy(source, slots.at[number], sems.at[number]))
        copies[number].start()
    total = refs[len(parts)][...] if carried else None
    for number, weight in enumerate(weights):
        copies[number].wait()
        term = nn(slots[number], weight[...])
        total = term if total is None else total + term
    first = 0
    for out in refs[len(parts) + carried : len(refs) - 2]:
        width = out.shape[1]
        out[...] = total[:, first : first + width].astype(out.dtype)
        first += width


def project(ids, hidden, weights, total, widths, dtype):
    rows, size = hidden.shape[0], weights[0][0].shape[0]
    arrays = [array for array, *_ in weights] + total
    parts = [part for _, part, _ in weights]
    return pl.pallas_call(
        functools.partial(project_kernel, parts, len(total)),
        out_shape=tuple(shape((rows, width), dtype) for width in widths),
        in_specs=[SMEM, ANY] + [VMEM] * len(arrays),
        out_specs=(VMEM,) * len(widths),
        scratch_shapes=[pltpu.VMEM((len(parts), rows, size), BF16), pltpu.SemaphoreType.DMA((len(parts),))],
        compiler_params=pltpu.CompilerParams(vmem_limit_bytes=16 * MIB),
        cost_estimate=pl.CostEstimate(
            flops=2 * rows * size * len(parts) * sum(widths), bytes_accessed=4 * MIB, transcendentals=0
        ),
        name="project",
    )(ids, in_hbm(hidden), *arrays)


def hidden_kernel(places, ids_ref, grad_ref, *refs):
    count = len(places)
    slots = refs[count + 1 :]
    copies = fetch(refs[:count], slots)
    size = sum(slots[i].shape[0] for i in range(count) if places[i][0] == 0)
    for i, (part, first) in enumerate(places):
        rows = slots[i].shape[0]
        start = pl.multiple_of(ids_ref[part] * size + first, rows)
        copies[i].wait()
        refs[count][:, pl.ds(start, rows)] = nt(grad_ref[...], slots[i][...]).astype(BF16)


def hidden_grad(ids, grad, weights, depth):
    return pallas(
        functools.partial(hidden_kernel, [place for _, *place in weights]),
        shape((grad.shape[0], depth)),
        [ids],
        [grad],
        "hidden_grad",
        2 * grad.size * depth,
        far=[array for array, *_ in weights],
    )


def attend_kernel(layouts, group, rows, bq, bk, block_ref, pages_ref, *refs):
    count = sum(len(layout) for layout in layouts)
    parts, (grad_ref, own_ref) = refs[:count], refs[count : count + 2]
    q_ref, k_ref, v_ref, do_ref, s_ref, dp_ref, dk_ref, dv_ref, kt_ref, m_ref = refs[count + 2 :]
    seq, hd = do_ref.shape
    near = rows * group
    block = block_ref[0]
    scale = hd**-0.5
    scale2 = scale * math.log2(math.e)
    at = 0
    for layout, targets in zip(layouts, ((q_ref, k_ref), (v_ref,), (do_ref,))):
        for distances in layout:
            for number, distance in enumerate(distances):
                here = pl.ds(pl.multiple_of((block ^ distance) * rows, rows), rows)
                for column, target in enumerate(targets):
                    target[here, :] = parts[at][number * rows : (number + 1) * rows, column * hd : (column + 1) * hd]
            at += 1
    dk_ref[...] = jnp.zeros_like(dk_ref)
    dv_ref[...] = jnp.zeros_like(dv_ref)
    kt_ref[...] = k_ref[...].T
    ends, end = [], jnp.int32(0)
    for page in range(pages_ref.shape[1]):
        end = end + pages_ref[0, page]
        ends.append(end)
    low = lax.div(block, group) * near
    near_first, near_last = lax.div(low, bk), lax.div(low, bk) + near // bk

    def limit_of(pos):
        limit = jnp.full_like(pos, seq)
        for page_end in ends:
            limit = jnp.minimum(limit, jnp.where(page_end > pos, page_end, seq))
        return limit

    @pl.loop(0, seq // bq)
    def _(i):
        q0 = pl.multiple_of(i * bq, bq)
        limits = limit_of(q0 + lax.broadcasted_iota(jnp.int32, (1, bq), 1))
        count = lax.div(limit_of(q0 + (bq - 1)) + (bk - 1), bk)
        first, last = jnp.minimum(near_first, count), jnp.minimum(near_last, count)
        is_near = (q0 >= low) & (q0 < low + near)

        @pl.when(is_near | (first < last))
        def _():
            q = q_ref[pl.ds(q0, bq), :]
            do = do_ref[pl.ds(q0, bq), :]
            qt, dot_t = q.T, do.T

            def scores(masked, j, carry):
                row_max, total, dot = carry
                k0 = pl.multiple_of(j * bk, bk)
                s = nn(k_ref[pl.ds(k0, bk), :], qt) * scale2
                if masked:
                    key = k0 + lax.broadcasted_iota(jnp.int32, (bk, 1), 0)
                    s = jnp.where(key < limits, s, -1e30)
                high = jnp.maximum(row_max, jnp.max(s, axis=0, keepdims=True))
                p = jnp.exp2(s - high)
                dp = nn(v_ref[pl.ds(k0, bk), :], dot_t)
                s_ref[pl.ds(k0, bk), :] = p
                dp_ref[pl.ds(k0, bk), :] = dp
                m_ref[j] = high
                fade = jnp.exp2(row_max - high)
                total = total * fade + jnp.sum(p, axis=0, keepdims=True)
                dot = dot * fade + jnp.sum(p * dp, axis=0, keepdims=True)
                return high, total, dot

            zero = jnp.zeros((1, bq), F32)
            carry = (jnp.full((1, bq), -3e38, F32), zero, zero)
            full = jnp.minimum(lax.div(q0, bk), count)
            carry = lax.fori_loop(0, full, functools.partial(scores, False), carry)
            row_max, total, dot = lax.fori_loop(full, count, functools.partial(scores, True), carry)
            inv = 1.0 / total
            dot = dot * inv

            def dscore(j):
                k0 = pl.multiple_of(j * bk, bk)
                share = jnp.exp2(m_ref[j] - row_max) * inv
                gain = share * scale
                p = s_ref[pl.ds(k0, bk), :]
                return k0, p * share, (p * (dp_ref[pl.ds(k0, bk), :] * gain - dot * gain)).astype(BF16)

            def key_grads(j, carry):
                k0, p, ds = dscore(j)
                dv_ref[pl.ds(k0 - low, bk), :] += nn(p.astype(BF16), do)
                dk_ref[pl.ds(k0 - low, bk), :] += nn(ds, q)
                return carry

            def query_grads(j, dqt):
                k0, _, ds = dscore(j)
                return dqt + nn(kt_ref[:, pl.ds(k0, bk)], ds)

            def all_grads(j, dqt):
                k0, p, ds = dscore(j)
                dv_ref[pl.ds(k0 - low, bk), :] += nn(p.astype(BF16), do)
                dk_ref[pl.ds(k0 - low, bk), :] += nn(ds, q)
                return dqt + nn(kt_ref[:, pl.ds(k0, bk)], ds)

            @pl.when(is_near)
            def _():
                dqt = lax.fori_loop(0, first, query_grads, jnp.zeros((hd, bq), F32))
                dqt = lax.fori_loop(first, last, all_grads, dqt)
                dqt = lax.fori_loop(last, count, query_grads, dqt)
                grad_ref[pl.ds(pl.multiple_of(q0 - low, bq), bq), :hd] = dqt.T.astype(BF16)

            @pl.when(jnp.logical_not(is_near))
            def _():
                lax.fori_loop(first, last, key_grads, 0)

    grad_ref[:, hd : 2 * hd] = dk_ref[...].astype(BF16)
    grad_ref[:, 2 * hd :] = dv_ref[...].astype(BF16)
    own = pl.multiple_of(lax.rem(block, group) * rows, rows)
    own_ref[...] = grad_ref[pl.ds(own, rows), :]


def attend(block, pages, sets, blocks, group):
    rows = sets[0][0][0].shape[0] // len(sets[0][0][1])
    hd = sets[1][0][0].shape[1]
    seq, near = rows * blocks, rows * group
    bq, bk = (near, 2 * rows) if seq <= 4096 else (rows, rows)
    layouts = [[distances for _, distances in parts] for parts in sets]
    return pallas(
        functools.partial(attend_kernel, layouts, group, rows, bq, bk),
        (shape((near, 3 * hd)), shape((rows, 3 * hd))),
        [block, pages],
        [array for parts in sets for array, _ in parts],
        "attend",
        10 * seq * seq * hd,
        [pltpu.VMEM((seq, hd), BF16)] * 4
        + [pltpu.VMEM((seq, bq), F32)] * 2
        + [pltpu.VMEM((near, hd), F32)] * 2
        + [pltpu.VMEM((hd, seq), BF16), pltpu.VMEM((seq // bk, 1, bq), F32)],
    )


def weight_kernel(group, piece, places, ids_ref, fsdp_ref, grad_ref, hidden_ref, *refs):
    parts, (kept_ref, away_ref, own_ref, sems) = refs[: len(places)], refs[len(places) :]
    copies = cut_copies([(0, 0)], [own_ref], group, piece, ids_ref, hidden_ref, sems)
    rows, width = own_ref.shape
    fsdp_size = 2 * kept_ref.shape[0]
    size = width // fsdp_size
    for copy in copies:
        copy.wait()
    for j in range(fsdp_size):
        columns = pl.ds(pl.multiple_of(fsdp_ref[j] * size, size), size)
        total = None
        for (k, first), part in zip([(0, 0), *places], (own_ref, *parts)):
            count = part.shape[0]
            here = pl.ds(pl.multiple_of(ids_ref[k] * rows + first, math.gcd(rows, first)), count)
            term = tn(part[:, columns], grad_ref[here, :])
            total = term if total is None else total + term
        out = away_ref if j % 2 else kept_ref
        out[j // 2] = total.astype(out.dtype)


def weight_grad(ids, fsdp_ids, grad, hidden, parts, group, piece):
    fsdp_size, width = fsdp_ids.shape[0], grad.shape[1]
    rows, columns = hidden.shape[0], parts[0][0].shape[1]
    size = columns // fsdp_size
    half = (fsdp_size // 2, size, width)
    if piece % 128:
        parts = [(cut_plain(ids, hidden, 0, group, piece), 0, 0), *parts]
        total = sum(
            tn(array, lax.dynamic_slice_in_dim(grad, ids[k] * rows + first, array.shape[0], 0))
            for array, k, first in parts
        )
        both = jnp.take(total.reshape(fsdp_size, size, width), fsdp_ids, axis=0)
        both = both.reshape(fsdp_size // 2, 2, size, width)
        return both[:, 0], both[:, 1].astype(BF16)
    return pl.pallas_call(
        functools.partial(weight_kernel, group, piece, [(k, first) for _, k, first in parts]),
        out_shape=(shape(half, F32), shape(half)),
        in_specs=[SMEM, SMEM, VMEM, ANY] + [VMEM] * len(parts),
        out_specs=(VMEM, VMEM),
        scratch_shapes=[pltpu.VMEM((rows, columns), BF16), pltpu.SemaphoreType.DMA((columns // piece,))],
        compiler_params=pltpu.CompilerParams(vmem_limit_bytes=20 * MIB),
        cost_estimate=pl.CostEstimate(flops=2 * grad.size * columns, bytes_accessed=8 * MIB, transcendentals=0),
        name="weight_grad",
    )(ids, fsdp_ids, grad, hidden, *[array for array, *_ in parts])


def finish_kernel(group, piece, turn, ids_ref, *refs):
    blocks, (out_ref, wide_ref, sems) = refs[:group], refs[len(refs) - 3 :]
    copies = []
    for number, block in enumerate(blocks):
        count = block.shape[0] // piece
        for i in range(count):
            place = (turn * count + i) * group + ids_ref[number]
            here = pl.ds(pl.multiple_of(place * piece, piece), piece)
            slot = wide_ref.at[len(copies)]
            slot[...] = block[i * piece : (i + 1) * piece, :].astype(F32)
            copies.append(pltpu.make_async_copy(slot, out_ref.at[here, :], sems.at[len(copies)]))
            copies[len(copies) - 1].start()
    for copy in copies:
        copy.wait()


def finish(ids, blocks, group, piece):
    rows, width = blocks[0].shape
    if piece % 16:
        order = jnp.stack(blocks).reshape(-1, group, rows // piece, piece, width)
        order = jnp.take(order, ids, axis=1).swapaxes(1, 2)
        return order.reshape(len(blocks) * rows, width).astype(F32)
    out = []
    for turn in range(len(blocks) // group):
        number = group * rows // piece
        out = pl.pallas_call(
            functools.partial(finish_kernel, group, piece, turn),
            out_shape=shape((len(blocks) * rows, width), F32),
            in_specs=[SMEM] + [VMEM] * group + [ANY] * (turn > 0),
            out_specs=ANY,
            input_output_aliases={group + 1: 0} if turn else {},
            scratch_shapes=[pltpu.VMEM((number, piece, width), F32), pltpu.SemaphoreType.DMA((number,))],
            compiler_params=pltpu.CompilerParams(vmem_limit_bytes=12 * MIB),
            cost_estimate=pl.CostEstimate(flops=0, bytes_accessed=3 * MIB, transcendentals=0),
            name="finish",
        )(ids, *blocks[turn * group : (turn + 1) * group], *([out] if turn else []))
    return out


def swap(array, axis, size, distance):
    return lax.ppermute(array, axis, [(i, i ^ distance) for i in range(size)])


def spread(part, size):
    array, distances = part
    return [(swap(array, "ctx", size, k), [k ^ d for d in distances]) for k in range(2, size, 2)]


def widen(parts, size):
    arrays = [array for array, _ in parts]
    whole = jnp.concatenate(arrays, axis=0) if len(arrays) > 1 else arrays[0]
    return swap(whole, "ctx", size, 1), [1 ^ d for _, distances in parts for d in distances]


def after(part, done):
    array, *_ = lax.optimization_barrier((part[0], *[other for other, _ in done]))
    return array, part[1]


def local(ctx_size, fsdp_size, hidden_in, page_tokens, grad_attn, w_qkv):
    hidden, grad_out = hidden_in[0], grad_attn[0]
    rows, depth = hidden.shape
    hd = grad_out.shape[1]
    f, c = lax.axis_index("fsdp"), lax.axis_index("ctx")
    fsdp_ids = f ^ jnp.arange(fsdp_size, dtype=jnp.int32)
    group = min(4, ctx_size)
    group_ids = (c % group) ^ jnp.arange(group, dtype=jnp.int32)

    piece = depth // (fsdp_size * ctx_size)
    top = fsdp_size // 2
    weights = {0: [w_qkv], top: [swap(w_qkv, "fsdp", fsdp_size, top)]}
    near = rows * 5 // 8
    members = [(1, 0, rows), (2, 0, near), (2, near, rows - near)]
    chunks = cut(group_ids, hidden, members[:2], group, piece)
    grads = [(grad_out, [0])]
    grads += spread(grads[0], ctx_size)
    moved = [swap(chunk, "ctx", ctx_size, k) for chunk, (k, *_) in zip(chunks[:2], members)]
    arrays, _ = lax.optimization_barrier(([array for array, _ in grads], chunks))
    grads = [(array, distances) for array, (_, distances) in zip(arrays, grads)]
    whole = jnp.concatenate([array for array, _ in grads], axis=0)
    array, distances = widen([(whole, [d for _, distances in grads for d in distances])], ctx_size)
    weights[1] = [swap(w_qkv, "fsdp", fsdp_size, 1)]
    early = [(weights[k][0], k, 0) for k in (0, 1)]
    (total,) = project(fsdp_ids, hidden, early, [], (3 * hd,), F32)
    weights[top], array, total = lax.optimization_barrier((weights[top], array, total))
    grads.append((array, distances))
    bit = top // 2
    while bit:
        for k in list(weights):
            if k ^ bit not in weights:
                weights[k ^ bit] = [swap(weights[k][0], "fsdp", fsdp_size, bit)]
        bit //= 2
    weights = [(weights[k][0], k, 0) for k in range(fsdp_size)]

    qk, v = project(fsdp_ids, hidden, weights[2:], [total], (2 * hd, hd), BF16)
    qks = [(qk, [0])]
    qks += spread(qks[0], ctx_size)
    v_pair = [(v, [0]), widen([after((v, [0]), [(moved[0], 0)])], ctx_size)]
    pair = jnp.concatenate([array for array, _ in v_pair], axis=0), [0, 1]
    vs = [pair, *spread(after(pair, qks[1:]), ctx_size)]
    qks.append(widen([after(qks[0], [pair, (moved[0], 0), (moved[1], 0)]), *qks[1:]], ctx_size))
    members.append((3, 0, rows))
    middle, late = cut(group_ids, after((hidden, 0), [(qk, 0)])[0], members[2:], group, piece)
    moved.append(swap(after((middle, 0), qks[1 : ctx_size // 2])[0], "ctx", ctx_size, 2))
    moved.append(swap(after((late, 0), [qks[-1], vs[1]])[0], "ctx", ctx_size, 3))
    block = c.reshape(1).astype(jnp.int32)
    grad_near, grad_own = attend(block, page_tokens, [qks, vs, grads], ctx_size, group)
    parts = [(array, k, first) for array, (k, first, _) in zip(moved, members)]
    kept, away = weight_grad(group_ids, fsdp_ids, grad_near, hidden, parts, group, piece)
    bit = 1
    while bit < top:
        total = kept + swap(away, "fsdp", fsdp_size, bit).astype(F32)
        bit *= 2
        kept, away = total[0::2], total[1::2].astype(BF16)
    half = kept.shape[1] // 2
    first = swap(away[0, :half], "fsdp", fsdp_size, top)
    second, first = lax.optimization_barrier((away[0, half:], first))
    second = swap(second, "fsdp", fsdp_size, top)
    totals = [kept[0, :half] + first.astype(F32)]
    rest, total = lax.optimization_barrier((kept[0, half:], totals[0].astype(BF16)))
    grad_own, total = lax.optimization_barrier((grad_own, total))
    grad_inputs = hidden_grad(fsdp_ids, grad_own, weights, depth)
    second, grad_inputs = lax.optimization_barrier((second, grad_inputs))
    totals = [total, rest + second.astype(F32)]
    bit = group
    while bit < ctx_size:
        sent = [total.astype(BF16) for total in totals]
        totals = [own.astype(F32) + swap(own, "ctx", ctx_size, bit).astype(F32) for own in sent]
        bit *= 2
    totals = [total.astype(BF16) for total in totals]
    gathered = [swap(total, "ctx", ctx_size, k) if k else total for total in totals for k in range(group)]
    grad_weights = finish(group_ids, gathered, group, piece)
    return grad_inputs[None], grad_weights


def solution(mesh):
    in_specs = (P("fsdp", "ctx", None), P("fsdp", None), P("fsdp", "ctx", None), P("fsdp", None))
    out_specs = (P("fsdp", "ctx", None), P("fsdp", None))
    body = functools.partial(local, mesh.shape["ctx"], mesh.shape["fsdp"])
    return jax.shard_map(body, mesh=mesh, in_specs=in_specs, out_specs=out_specs, check_vma=False)
```
